32 devices in a mesh: row: 2 (over y), col: 4 (over z), batch: 4 (over x, core).
Axes of the slice: x: 2, y: 2, z: 4, core: 2. Of those that a mesh axis runs over, the one named last changes fastest.
Arguments:
- features: bfloat16 [4096, 8192], P(('col', 'batch'), 'row'), may hold values from -6 to 6
- cross_weight: bfloat16 [8192, 8192], P('row', ('col', 'batch')), may hold values from -0.09375 to 0.09375
- cross_bias: float32 [8192], P('col'), may hold values from -3 to 3
- pattern: int32 [16, 16], replicated, may hold values from 0 to 1, as said below
- linear_weight: bfloat16 [8192, 8192], P('col', ('row', 'batch')), may hold values from -0.0625 to 0.0625
- linear_bias: float32 [8192], P('row'), may hold values from -3 to 3
Outputs:
- mixed_out: bfloat16 [4096, 8192], P(('col', 'batch'), 'row')
The draws below stay inside these ranges and needn't reach their ends.
Inputs may be any that keep to these rules, and one draw needn't show every extreme that they name: `pattern`: entries are 0 or 1; exactly half of the 16 x 16 blocks are 1.
All inputs are finite; a program needn't handle non-finite values.
Results may differ from the reference program's by a relative error of at most 0.019.
Values may be sent and summed in bfloat16 or wider, within the bound.
No kernel may reach another device: no remote copies, remote signals or barrier semaphores. Data moves between devices by JAX's collectives and lax.ppermute only.
A program may use at most 128 MiB of HBM per device.

```python
import jax
import jax.numpy as jnp
from jax import lax

D = 8192
NB = 16
SAMPLES = 4096
N_ROW = 2
N_COL = 4


def draw_pattern(key, part):
    order = jax.random.permutation(jax.random.fold_in(key, 7), NB * NB)
    kept_cells = (order < NB * NB // 2).astype(jnp.int32)
    return kept_cells.reshape(NB, NB)


def shard_levels(stream_key, dims, shards, low, top_value):
    def one(dim, parts):
        steps = jax.random.uniform(jax.random.fold_in(jax.random.fold_in(stream_key, 6), dim), (parts,), jnp.float32, low / len(shards), top_value / len(shards))
        return jnp.repeat(jnp.exp(steps), dims[dim] // parts).reshape((-1,) + (1,) * (len(dims) - dim - 1))

    gain = one(*shards[0])
    for cut in shards[1:]:
        gain = gain * one(*cut)
    return gain


def centred(rng, extent, width, reach, cuts=(), held_as=jnp.bfloat16):
    values = width * jax.random.normal(rng, extent, jnp.float32)
    if cuts:
        values = values * shard_levels(rng, extent, cuts, -0.22, 0.18)
    return jnp.clip(values, -reach, reach).astype(held_as)


def setup_inputs(seed: int = 0) -> dict:
    streams_of = jax.random.split(jax.random.key(seed), 7)
    return {
        "features": centred(streams_of[0], (SAMPLES, D), 1.0, 6.0, ((0, 16), (1, 2))),
        "cross_weight": centred(streams_of[1], (D, D), (D // 2) ** -0.5, 0.09375, ((0, 2), (1, 16))),
        "cross_bias": centred(streams_of[2], (D,), 0.5, 3.0, ((0, 4),), jnp.float32),
        "pattern": draw_pattern(jax.random.fold_in(streams_of[6], 71), 0),
        "linear_weight": centred(streams_of[4], (D, D), D ** -0.5, 0.0625, ((0, 4), (1, 8))),
        "linear_bias": centred(streams_of[5], (D,), 0.5, 3.0, ((0, 2),), jnp.float32),
    }


def grouped_product(left_side, right_side, groups):
    group_width = left_side.shape[1] // groups

    def add_group(running, group_index):
        first = (group_index * group_width).astype(jnp.int32)
        left_cols = lax.dynamic_slice_in_dim(left_side, first, group_width, 1)
        right_rows = lax.dynamic_slice_in_dim(right_side, first, group_width, 0)
        rounded = jnp.dot(left_cols, right_rows, preferred_element_type=jnp.float32).astype(jnp.bfloat16)
        return running + rounded.astype(jnp.float32), None

    start_sum = jnp.zeros((left_side.shape[0], right_side.shape[1]), jnp.float32)
    running, _ = lax.scan(add_group, start_sum, jnp.arange(groups, dtype=jnp.int32))
    return running


def reference(features, cross_weight, cross_bias, pattern, linear_weight, linear_bias):
    block_size = D // NB
    kept_mask = pattern.T.astype(cross_weight.dtype)
    pruned = (cross_weight.reshape(NB, block_size, NB, block_size) * kept_mask[:, None, :, None]).reshape(D, D)
    hidden = grouped_product(features, pruned, N_ROW)
    base = features.astype(jnp.float32)
    crossed = (base * (hidden + cross_bias) + base).astype(jnp.bfloat16)
    summed = grouped_product(crossed, linear_weight, N_COL)
    return (summed + linear_bias).astype(jnp.bfloat16)
```

```python
import jax
import jax.numpy as jnp
from jax import lax
from jax.sharding import PartitionSpec as P

CHUNKS = 2


def axis_pairs(size, bit):
    return [(place, place ^ bit) for place in range(size)]


def gather_pieces(shard, size):
    pieces = {0: shard}
    bit = size // 2
    while bit:
        for apart in list(pieces):
            pieces[apart | bit] = lax.ppermute(pieces[apart], "batch", axis_pairs(size, bit))
        bit //= 2
    return pieces


def build(mesh):
    n_row, n_col, n_batch = (mesh.shape[name] for name in ("row", "col", "batch"))

    def on_device(features, cross_weight, cross_bias, pattern, linear_weight, linear_bias):
        grid_side = pattern.shape[0]
        input_width = cross_weight.shape[0]
        width = input_width * n_row
        piece_width = cross_weight.shape[1]
        output_width = piece_width * n_batch
        mixed_width = linear_weight.shape[1]
        block_size = width // grid_side
        row, col, batch = (lax.axis_index(name) for name in ("row", "col", "batch"))

        out_of = (col * n_batch + batch) * piece_width + jnp.arange(piece_width)
        in_of = row * input_width + jnp.arange(input_width)
        kept_columns = jnp.take(pattern, out_of // block_size, axis=0)
        kept = jnp.take(kept_columns, in_of // block_size, axis=1).T
        pruned = cross_weight * kept.astype(cross_weight.dtype)

        cross_pieces = gather_pieces(pruned, n_batch)
        linear_shard, cross_pieces[n_batch // 2] = lax.optimization_barrier(
            (linear_weight, cross_pieces[n_batch // 2])
        )
        linear_pieces = {}
        near = range(n_batch // 2)
        far = range(n_batch // 2, n_batch)
        linear_pieces = gather_pieces(linear_shard, n_batch)
        linear_groups = [
            (group, jnp.concatenate([linear_pieces[apart] for apart in group], axis=1))
            for group in (near, far)
        ]

        rows_per = features.shape[0] // CHUNKS
        gathered = [
            lax.all_gather(
                features[step * rows_per : (step + 1) * rows_per], "col", axis=0, tiled=True
            )
            for step in range(CHUNKS)
        ]

        def owner_of(column):
            return column * output_width // input_width

        is_owner = row == col * output_width // input_width
        turns = []
        for turn in range(1, n_row):
            turns.append(
                [
                    (((owner_of(c) + turn) % n_row) * n_col + c, owner_of(c) * n_col + c)
                    for c in range(n_col)
                ]
            )
        first_base = jnp.where(is_owner, col * output_width - row * input_width, 0)

        crossed = []
        for samples in gathered:
            whole = jnp.zeros((samples.shape[0], output_width), jnp.bfloat16)
            for apart in range(n_batch):
                first = (batch ^ apart) * piece_width
                own = jnp.dot(samples, cross_pieces[apart], preferred_element_type=jnp.float32)
                own = own.astype(jnp.bfloat16)
                hidden = own.astype(jnp.float32)
                for pairs in turns:
                    hidden = hidden + lax.ppermute(own, ("row", "col"), pairs).astype(jnp.float32)
                base = lax.dynamic_slice_in_dim(
                    samples, first_base + first, piece_width, 1
                ).astype(jnp.float32)
                bias = lax.dynamic_slice_in_dim(cross_bias, first, piece_width)
                mine = (base * (hidden + bias) + base).astype(jnp.bfloat16)
                theirs = jnp.zeros_like(mine)
                for pairs in turns:
                    theirs = theirs + lax.ppermute(
                        mine, ("row", "col"), [(to, came) for came, to in pairs]
                    )
                whole = lax.dynamic_update_slice_in_dim(
                    whole, jnp.where(is_owner, mine, theirs), first, 1
                )
            crossed.append(whole)

        out = jnp.zeros((features.shape[0], mixed_width * n_batch), jnp.bfloat16)
        for group, weight in linear_groups:
            for step, whole in enumerate(crossed):
                partial = jnp.dot(whole, weight, preferred_element_type=jnp.float32)
                summed = lax.psum_scatter(
                    partial.astype(jnp.bfloat16), "col", scatter_dimension=0, tiled=True
                ).astype(jnp.float32)
                for place, apart in enumerate(group):
                    first = (batch ^ apart) * mixed_width
                    bias = lax.dynamic_slice_in_dim(linear_bias, first, mixed_width)
                    part = summed[:, place * mixed_width : (place + 1) * mixed_width] + bias
                    out = lax.dynamic_update_slice(
                        out, part.astype(jnp.bfloat16), (step * rows_per, first)
                    )
        return out

    return on_device


def solution(mesh):
    return jax.shard_map(
        build(mesh),
        mesh=mesh,
        in_specs=(
            P(("col", "batch"), "row"),
            P("row", ("col", "batch")),
            P("col"),
            P(),
            P("col", ("row", "batch")),
            P("row"),
        ),
        out_specs=P(("col", "batch"), "row"),
        check_vma=False,
    )
```

```python
import functools

import jax
import jax.numpy as jnp
from jax import lax
from jax.experimental import pallas as pl
from jax.experimental.pallas import tpu as pltpu
from jax.sharding import PartitionSpec as P

SHARES = (4, 4)
VMEM_BYTES = 48 * 2**20


def far_and_near(size, bit):
    return [(place, place ^ bit) for place in range(size)]


def cross_kernel(meta, samples, weight, out, total):
    step = pl.program_id(0)

    @pl.when(step == 0)
    def _():
        total[...] = jnp.zeros_like(total)

    @pl.when(step < meta[0])
    def _():
        total[...] += jnp.dot(samples[...], weight[...], preferred_element_type=jnp.float32)

    @pl.when(step == pl.num_programs(0) - 1)
    def _():
        out[...] = total[...].astype(out.dtype)


def cross_product(meta, samples, weight, block):
    rows, depth = samples.shape
    columns = weight.shape[1]
    steps = depth // block
    return pl.pallas_call(
        cross_kernel,
        out_shape=jax.ShapeDtypeStruct((rows, columns), jnp.bfloat16),
        grid_spec=pltpu.PrefetchScalarGridSpec(
            num_scalar_prefetch=1,
            grid=(steps,),
            in_specs=[
                pl.BlockSpec((rows, block), lambda i, meta: (0, meta[1 + i])),
                pl.BlockSpec((block, columns), lambda i, meta: (meta[1 + i], 0)),
            ],
            out_specs=pl.BlockSpec((rows, columns), lambda i, meta: (0, 0)),
            scratch_shapes=[pltpu.VMEM((rows, columns), jnp.float32)],
        ),
        compiler_params=pltpu.CompilerParams(vmem_limit_bytes=VMEM_BYTES),
        cost_estimate=pl.CostEstimate(
            flops=rows * depth * columns,
            bytes_accessed=(rows * depth + depth * columns + 2 * rows * columns),
            transcendentals=0,
        ),
    )(meta, samples, weight)


def linear_kernel(count, per_piece, meta, *refs):
    mine, theirs = refs[:count], refs[count : 2 * count]
    weights, out, joined = refs[2 * count : -2], refs[-2], refs[-1]
    step = pl.program_id(0)

    @pl.when(step == 0)
    def _():
        for apart in range(count):
            width = mine[apart].shape[1]
            columns = pl.ds(pl.multiple_of(meta[1 + apart] * width, width), width)

            @pl.when(meta[0] == 1)
            def _():
                joined[:, columns] = mine[apart][...]

            @pl.when(meta[0] == 0)
            def _():
                joined[:, columns] = theirs[apart][...]

    for place, weight in enumerate(weights):

        @pl.when(step // per_piece == place)
        def _():
            out[...] = jnp.dot(
                joined[...], weight[...], preferred_element_type=jnp.float32
            ).astype(out.dtype)


def linear_product(meta, mine, theirs, weights):
    count = len(mine)
    rows, width = mine[0].shape
    depth, columns = weights[0].shape
    tile = min(columns, 512)
    per_piece = columns // tile
    part = pl.BlockSpec((rows, width), lambda i, meta: (0, 0))

    def weight_spec(place):
        return pl.BlockSpec(
            (depth, tile),
            lambda i, meta: (0, jnp.clip(i - place * per_piece, 0, per_piece - 1)),
        )

    def out_index(i, meta):
        return 0, meta[1 + count + i // per_piece] * per_piece + i % per_piece

    return pl.pallas_call(
        functools.partial(linear_kernel, count, per_piece),
        out_shape=jax.ShapeDtypeStruct((rows, columns * len(weights)), jnp.bfloat16),
        grid_spec=pltpu.PrefetchScalarGridSpec(
            num_scalar_prefetch=1,
            grid=(per_piece * len(weights),),
            in_specs=[part] * (2 * count) + [weight_spec(p) for p in range(len(weights))],
            out_specs=pl.BlockSpec((rows, tile), out_index),
            scratch_shapes=[pltpu.VMEM((rows, depth), jnp.bfloat16)],
        ),
        compiler_params=pltpu.CompilerParams(vmem_limit_bytes=VMEM_BYTES),
        cost_estimate=pl.CostEstimate(
            flops=2 * rows * depth * columns * len(weights),
            bytes_accessed=4 * rows * depth
            + 2 * (depth + rows) * columns * len(weights),
            transcendentals=0,
        ),
    )(meta, *mine, *theirs, *weights)


def after(value, *others):
    return lax.optimization_barrier((value, *others))[0]


def added(*terms):
    return sum(term.astype(jnp.float32) for term in terms)


def finish_kernel(meta, own, came, samples, bias, out):
    base = samples[...].astype(jnp.float32)
    hidden = own[...].astype(jnp.float32) + came[...].astype(jnp.float32)
    out[...] = (base * (hidden + bias[...]) + base).astype(out.dtype)


def finish_cross(meta, own, came, samples, bias):
    rows, columns = own.shape
    tile = rows // 2
    part = pl.BlockSpec((tile, columns), lambda i, meta: (i, 0))
    return pl.pallas_call(
        finish_kernel,
        out_shape=jax.ShapeDtypeStruct((rows, columns), jnp.bfloat16),
        grid_spec=pltpu.PrefetchScalarGridSpec(
            num_scalar_prefetch=1,
            grid=(2,),
            in_specs=[
                part,
                part,
                pl.BlockSpec((tile, columns), lambda i, meta: (i, meta[0])),
                pl.BlockSpec((1, columns), lambda i, meta: (0, meta[1])),
            ],
            out_specs=part,
        ),
        cost_estimate=pl.CostEstimate(
            flops=4 * rows * columns, bytes_accessed=8 * rows * columns, transcendentals=0
        ),
    )(meta, own, came, samples, bias)


class LineSum:
    def __init__(self, partial, place, size):
        self.partial, self.place, self.size = partial, place, size
        self.rows = partial.shape[0] // size
        self.begun = []
        if size == 4:
            inward = [(0, 1), (3, 2)]
            self.begun = [lax.ppermute(self.part(i), "col", inward) for i in (3, 2, 1)]

    def part(self, if_lower):
        upper = self.place >= self.size // 2
        first = jnp.where(upper, self.size - 1 - if_lower, if_lower) * self.rows
        return lax.dynamic_slice_in_dim(self.partial, first, self.rows, 0)

    def end(self):
        if self.size != 4:
            summed = lax.psum_scatter(self.partial, "col", scatter_dimension=0, tiled=True)
            return summed.astype(jnp.float32)
        across, outward = [(1, 2), (2, 1)], [(1, 0), (2, 3)]
        from_3, from_2, from_1 = self.begun
        over_3 = lax.ppermute(added(self.part(3), from_3).astype(jnp.bfloat16), "col", across)
        over_2 = lax.ppermute(added(self.part(2), from_2).astype(jnp.bfloat16), "col", across)
        out_0 = lax.ppermute(added(self.part(0), over_3).astype(jnp.bfloat16), "col", outward)
        own = lax.dynamic_slice_in_dim(self.partial, self.place * self.rows, self.rows, 0)
        is_end = (self.place == 0) | (self.place == self.size - 1)
        return added(own) + jnp.where(is_end, added(out_0), added(from_1, over_2))


def build(mesh):
    n_row, n_col, n_batch = (mesh.shape[name] for name in ("row", "col", "batch"))

    def on_device(features, cross_weight, cross_bias, pattern, linear_weight, linear_bias):
        input_width, piece_width = cross_weight.shape
        width = input_width * n_row
        output_width = piece_width * n_batch
        mixed_width = linear_weight.shape[1]
        block = width // pattern.shape[0]
        in_blocks = input_width // block
        row, col, batch = (lax.axis_index(name) for name in ("row", "col", "batch"))
        half = n_batch // 2

        def to_batch(shard, bit):
            return lax.ppermute(shard, "batch", far_and_near(n_batch, bit))

        def spread_near(pieces):
            bit = half // 2
            while bit:
                for apart in list(pieces):
                    pieces[apart | bit] = to_batch(pieces[apart], bit)
                bit //= 2
            return pieces

        cross_across = to_batch(cross_weight, half)
        linear_across = to_batch(linear_weight, half)
        cross_pieces = spread_near({0: cross_weight})
        linear_pieces = spread_near({0: linear_weight})

        shard_rows = features.shape[0]
        starts = [shard_rows * sum(SHARES[:i]) // sum(SHARES) for i in range(len(SHARES) + 1)]
        gathered = [
            lax.all_gather(features[first:last], "col", axis=0, tiled=True)
            for first, last in zip(starts, starts[1:])
        ]

        def kept_list(apart):
            out_block = (col * n_batch + (batch ^ apart)) * piece_width // block
            kept = lax.dynamic_slice(pattern, (out_block, row * in_blocks), (1, in_blocks))[0]
            number = jnp.sum(kept)
            rank = jnp.cumsum(kept) - 1
            slots = jnp.minimum(jnp.arange(in_blocks), jnp.maximum(number - 1, 0))
            match = (rank[None, :] == slots[:, None]) & (kept[None, :] == 1)
            listed = jnp.sum(jnp.where(match, jnp.arange(in_blocks)[None, :], 0), axis=1)
            return jnp.concatenate([number[None], listed]).astype(jnp.int32)

        kept_lists = [kept_list(apart) for apart in range(n_batch)]

        def owner_of(column):
            return column * output_width // input_width

        is_owner = row == col * output_width // input_width
        turns = [
            [
                ((owner_of(c) + turn) % n_row * n_col + c, owner_of(c) * n_col + c)
                for c in range(n_col)
            ]
            for turn in range(1, n_row)
        ]
        first_base = jnp.where(is_owner, col * output_width - row * input_width, 0)

        chunks = range(len(SHARES))
        bias_row = cross_bias[None, :]
        near = [place for place in range(half)]
        far = [half + place for place in range(half)]
        products, mine, theirs = {}, {}, {}

        def multiply(step, group):
            for apart in group:
                products[step, apart] = cross_product(
                    kept_lists[apart], gathered[step], cross_pieces[apart], block
                )
            return [products[step, apart] for apart in group]

        def finish(step, group):
            for apart in group:
                first = (batch ^ apart) * piece_width
                own = products[step, apart]
                came = [lax.ppermute(own, ("row", "col"), pairs) for pairs in turns]
                place = jnp.stack([(first_base + first) // piece_width, batch ^ apart])
                crossed = finish_cross(
                    place.astype(jnp.int32), own, sum(came[1:], came[0]), gathered[step], bias_row
                )
                back = [
                    lax.ppermute(crossed, ("row", "col"), [(to, source) for source, to in pairs])
                    for pairs in turns
                ]
                mine[step, apart] = crossed
                theirs[step, apart] = sum(back[1:], back[0])

        meta = jnp.stack(
            [is_owner.astype(jnp.int32)]
            + [batch ^ place for place in range(n_batch)]
            + [(batch ^ place) % half for place in range(half)]
        ).astype(jnp.int32)

        def linear(step, group):
            return linear_product(
                meta,
                [mine[step, apart] for apart in range(n_batch)],
                [theirs[step, apart] for apart in range(n_batch)],
                [linear_pieces[apart] for apart in group],
            )

        sums = {}
        for step in chunks:
            last = step == chunks[-1]
            if step:
                gathered[step] = after(gathered[step], *sums[step - 1, 0].begun)
            sent = multiply(step, near)
            if not step:
                cross_across = after(cross_across, *sent)
                arrived = spread_near({0: cross_across})
                cross_pieces.update({half + place: arrived[place] for place in near})
            sent = multiply(step, far)
            if last:
                linear_across = after(linear_across, *sent)
                arrived = spread_near({0: linear_across})
                linear_pieces.update({half + place: arrived[place] for place in near})
                for past in range(step):
                    sums[past, 1] = LineSum(linear(past, far), col, n_col)
            finish(step, near + far)
            if last and step:
                mine[step, 0] = after(mine[step, 0], *sums[step - 1, 1].begun[:2])
            sums[step, 0] = LineSum(linear(step, near), col, n_col)
            if last:
                sums[step, 1] = LineSum(linear(step, far), col, n_col)

        out = jnp.zeros((shard_rows, mixed_width * n_batch), jnp.bfloat16)
        for step in chunks:
            for group in range(2):
                first = ((batch // half) ^ group) * half * mixed_width
                bias = lax.dynamic_slice_in_dim(linear_bias, first, half * mixed_width)
                out = lax.dynamic_update_slice(
                    out,
                    (sums[step, group].end() + bias).astype(jnp.bfloat16),
                    (starts[step], first),
                )
        return out

    return on_device


def solution(mesh):
    return jax.shard_map(
        build(mesh),
        mesh=mesh,
        in_specs=(
            P(("col", "batch"), "row"),
            P("row", ("col", "batch")),
            P("col"),
            P(),
            P("col", ("row", "batch")),
            P("row"),
        ),
        out_specs=P(("col", "batch"), "row"),
        check_vma=False,
    )
```

```python
import functools

import jax
import jax.numpy as jnp
from jax import lax
from jax.experimental import pallas as pl
from jax.experimental.pallas import tpu as pltpu
from jax.sharding import PartitionSpec as P

SHARES = (2, 3, 3)
VMEM_BYTES = 48 * 2**20


def far_and_near(size, bit):
    return [(place, place ^ bit) for place in range(size)]


def cross_kernel(meta, samples, weight, out, total):
    step = pl.program_id(0)

    @pl.when(step == 0)
    def _():
        total[...] = jnp.zeros_like(total)

    @pl.when(step < meta[0])
    def _():
        total[...] += jnp.dot(samples[...], weight[...], preferred_element_type=jnp.float32)

    @pl.when(step == pl.num_programs(0) - 1)
    def _():
        out[...] = total[...].astype(out.dtype)


def cross_product(meta, samples, weight, block):
    rows, depth = samples.shape
    columns = weight.shape[1]
    steps = depth // block
    return pl.pallas_call(
        cross_kernel,
        out_shape=jax.ShapeDtypeStruct((rows, columns), jnp.bfloat16),
        grid_spec=pltpu.PrefetchScalarGridSpec(
            num_scalar_prefetch=1,
            grid=(steps,),
            in_specs=[
                pl.BlockSpec((rows, block), lambda i, meta: (0, meta[1 + i])),
                pl.BlockSpec((block, columns), lambda i, meta: (meta[1 + i], 0)),
            ],
            out_specs=pl.BlockSpec((rows, columns), lambda i, meta: (0, 0)),
            scratch_shapes=[pltpu.VMEM((rows, columns), jnp.float32)],
        ),
        compiler_params=pltpu.CompilerParams(vmem_limit_bytes=VMEM_BYTES),
        cost_estimate=pl.CostEstimate(
            flops=rows * depth * columns,
            bytes_accessed=(rows * depth + depth * columns + 2 * rows * columns),
            transcendentals=0,
        ),
    )(meta, samples, weight)


def linear_kernel(count, per_piece, meta, *refs):
    mine, theirs = refs[:count], refs[count : 2 * count]
    weights, out, joined = refs[2 * count : -2], refs[-2], refs[-1]
    step = pl.program_id(0)

    @pl.when(step == 0)
    def _():
        for apart in range(count):
            width = mine[apart].shape[1]
            columns = pl.ds(pl.multiple_of(meta[1 + apart] * width, width), width)

            @pl.when(meta[0] == 1)
            def _():
                joined[:, columns] = mine[apart][...]

            @pl.when(meta[0] == 0)
            def _():
                joined[:, columns] = theirs[apart][...]

    for place, weight in enumerate(weights):

        @pl.when(step // per_piece == place)
        def _():
            out[...] = jnp.dot(
                joined[...], weight[...], preferred_element_type=jnp.float32
            ).astype(out.dtype)


def linear_product(meta, mine, theirs, weights):
    count = len(mine)
    rows, width = mine[0].shape
    depth, columns = weights[0].shape
    tile = min(columns, 512)
    per_piece = columns // tile
    part = pl.BlockSpec((rows, width), lambda i, meta: (0, 0))

    def weight_spec(place):
        return pl.BlockSpec(
            (depth, tile),
            lambda i, meta: (0, jnp.clip(i - place * per_piece, 0, per_piece - 1)),
        )

    def out_index(i, meta):
        return 0, meta[1 + count + i // per_piece] * per_piece + i % per_piece

    return pl.pallas_call(
        functools.partial(linear_kernel, count, per_piece),
        out_shape=jax.ShapeDtypeStruct((rows, columns * len(weights)), jnp.bfloat16),
        grid_spec=pltpu.PrefetchScalarGridSpec(
            num_scalar_prefetch=1,
            grid=(per_piece * len(weights),),
            in_specs=[part] * (2 * count) + [weight_spec(p) for p in range(len(weights))],
            out_specs=pl.BlockSpec((rows, tile), out_index),
            scratch_shapes=[pltpu.VMEM((rows, depth), jnp.bfloat16)],
        ),
        compiler_params=pltpu.CompilerParams(vmem_limit_bytes=VMEM_BYTES),
        cost_estimate=pl.CostEstimate(
            flops=2 * rows * depth * columns * len(weights),
            bytes_accessed=4 * rows * depth
            + 2 * (depth + rows) * columns * len(weights),
            transcendentals=0,
        ),
    )(meta, *mine, *theirs, *weights)


def after(value, *others):
    return lax.optimization_barrier((value, *others))[0]


def added(*terms):
    return sum(term.astype(jnp.float32) for term in terms)


def finish_kernel(meta, own, came, samples, bias, out):
    base = samples[...].astype(jnp.float32)
    hidden = own[...].astype(jnp.float32) + came[...].astype(jnp.float32)
    out[...] = (base * (hidden + bias[...]) + base).astype(out.dtype)


def finish_cross(meta, own, came, samples, bias):
    rows, columns = own.shape
    tile = rows // 2
    part = pl.BlockSpec((tile, columns), lambda i, meta: (i, 0))
    return pl.pallas_call(
        finish_kernel,
        out_shape=jax.ShapeDtypeStruct((rows, columns), jnp.bfloat16),
        grid_spec=pltpu.PrefetchScalarGridSpec(
            num_scalar_prefetch=1,
            grid=(2,),
            in_specs=[
                part,
                part,
                pl.BlockSpec((tile, columns), lambda i, meta: (i, meta[0])),
                pl.BlockSpec((1, columns), lambda i, meta: (0, meta[1])),
            ],
            out_specs=part,
        ),
        cost_estimate=pl.CostEstimate(
            flops=4 * rows * columns, bytes_accessed=8 * rows * columns, transcendentals=0
        ),
    )(meta, own, came, samples, bias)


class LineGather:
    def __init__(self, shard, place):
        self.shard, self.place = shard, place
        self.beside = lax.ppermute(shard, "col", [(0, 1), (1, 0), (2, 3), (3, 2)])
        self.over = lax.ppermute(shard, "col", [(1, 2), (2, 1)])

    def relay(self):
        outward = [(1, 0), (2, 3)]
        self.out = lax.ppermute(self.over, "col", outward)
        self.over_beside = lax.ppermute(self.beside, "col", [(1, 2), (2, 1)])
        self.out_beside = lax.ppermute(self.over_beside, "col", outward)

    def whole(self):
        place, shard = self.place, self.shard
        is_end = (place == 0) | (place == 3)
        lower = place < 2
        rows = shard.shape[0]
        whole = jnp.zeros((4 * rows, shard.shape[1]), shard.dtype)
        for part, at in (
            (shard, place),
            (self.beside, place ^ 1),
            (jnp.where(is_end, self.out, self.over), jnp.where(lower, 2, 1)),
            (jnp.where(is_end, self.out_beside, self.over_beside), jnp.where(lower, 3, 0)),
        ):
            whole = lax.dynamic_update_slice_in_dim(whole, part, at * rows, 0)
        return whole


class PlainGather:
    def __init__(self, shard, place):
        self.shard = self.beside = self.over = self.out = self.over_beside = self.out_beside = shard

    def relay(self):
        pass

    def whole(self):
        return lax.all_gather(self.shard, "col", axis=0, tiled=True)


def build(mesh):
    n_row, n_col, n_batch = (mesh.shape[name] for name in ("row", "col", "batch"))

    def on_device(features, cross_weight, cross_bias, pattern, linear_weight, linear_bias):
        input_width, piece_width = cross_weight.shape
        width = input_width * n_row
        output_width = piece_width * n_batch
        mixed_width = linear_weight.shape[1]
        block = width // pattern.shape[0]
        in_blocks = input_width // block
        row, col, batch = (lax.axis_index(name) for name in ("row", "col", "batch"))
        half = n_batch // 2

        def to_batch(shard, bit):
            return lax.ppermute(shard, "batch", far_and_near(n_batch, bit))

        def spread_near(pieces):
            bit = half // 2
            while bit:
                for apart in list(pieces):
                    pieces[apart | bit] = to_batch(pieces[apart], bit)
                bit //= 2
            return pieces

        cross_across = to_batch(cross_weight, half)
        linear_across = to_batch(linear_weight, half)
        cross_pieces = spread_near({0: cross_weight})
        linear_pieces = spread_near({0: linear_weight})

        shard_rows = features.shape[0]
        starts = [shard_rows * sum(SHARES[:i]) // sum(SHARES) for i in range(len(SHARES) + 1)]
        shards = [features[first:last] for first, last in zip(starts, starts[1:])]
        gathers, gathered = [], {}
        for step, shard in enumerate(shards):
            if step > 1:
                shard = after(shard, gathers[step - 2].beside)
            gathers.append((LineGather if n_col == 4 else PlainGather)(shard, col))

        def kept_list(apart):
            out_block = (col * n_batch + (batch ^ apart)) * piece_width // block
            kept = lax.dynamic_slice(pattern, (out_block, row * in_blocks), (1, in_blocks))[0]
            number = jnp.sum(kept)
            rank = jnp.cumsum(kept) - 1
            slots = jnp.minimum(jnp.arange(in_blocks), jnp.maximum(number - 1, 0))
            match = (rank[None, :] == slots[:, None]) & (kept[None, :] == 1)
            listed = jnp.sum(jnp.where(match, jnp.arange(in_blocks)[None, :], 0), axis=1)
            return jnp.concatenate([number[None], listed]).astype(jnp.int32)

        kept_lists = [kept_list(apart) for apart in range(n_batch)]

        def owner_of(column):
            return column * output_width // input_width

        is_owner = row == col * output_width // input_width
        turns = [
            [
                ((owner_of(c) + turn) % n_row * n_col + c, owner_of(c) * n_col + c)
                for c in range(n_col)
            ]
            for turn in range(1, n_row)
        ]
        first_base = jnp.where(is_owner, col * output_width - row * input_width, 0)

        chunks = range(len(SHARES))
        bias_row = cross_bias[None, :]
        near = [place for place in range(half)]
        far = [half + place for place in range(half)]
        products, came, mine, theirs = {}, {}, {}, {}

        latest = []

        def in_turn(meta, *others):
            return after(meta, *latest[-1:], *others)

        def multiply(step, group, *others):
            for apart in group:
                products[step, apart] = cross_product(
                    in_turn(kept_lists[apart], *others), gathered[step], cross_pieces[apart], block
                )
                latest.append(products[step, apart])
                came[step, apart] = [
                    lax.ppermute(products[step, apart], ("row", "col"), pairs) for pairs in turns
                ]

        def finish(step, group, *others):
            for apart in group:
                first = (batch ^ apart) * piece_width
                own, sent = products[step, apart], came[step, apart]
                place = jnp.stack([(first_base + first) // piece_width, batch ^ apart])
                crossed = finish_cross(
                    in_turn(place.astype(jnp.int32), *others), own, sum(sent[1:], sent[0]), gathered[step], bias_row
                )
                back = [
                    lax.ppermute(crossed, ("row", "col"), [(to, source) for source, to in pairs])
                    for pairs in turns
                ]
                mine[step, apart] = crossed
                latest.append(crossed)
                theirs[step, apart] = sum(back[1:], back[0])

        meta = jnp.stack(
            [is_owner.astype(jnp.int32)]
            + [batch ^ place for place in range(n_batch)]
            + [(batch ^ place) % half for place in range(half)]
        ).astype(jnp.int32)

        partial = {}

        def linear(step, group, *others):
            partial[step, group[0] // half] = linear_product(
                in_turn(meta, *others),
                [mine[step, apart] for apart in range(n_batch)],
                [theirs[step, apart] for apart in range(n_batch)],
                [linear_pieces[apart] for apart in group],
            )
            latest.append(partial[step, group[0] // half])

        first, second, third = gathers
        for gather in gathers:
            gather.relay()
        gathered.update({step: gather.whole() for step, gather in enumerate(gathers)})
        multiply(0, near, second.beside, second.over)
        finish(0, near, third.beside, second.out, second.over_beside)
        cross_across = after(cross_across, latest[-1], second.out_beside, third.over)
        arrived = spread_near({0: cross_across})
        cross_pieces.update({half + place: arrived[place] for place in near})
        multiply(0, far[:1], gathered[1])
        multiply(0, far[1:])
        multiply(1, near)
        finish(0, far, third.out, third.over_beside)
        multiply(1, far)
        finish(1, near)
        linear(0, near)
        multiply(2, near)
        finish(1, far)
        multiply(2, far)
        linear(1, near)
        finish(2, near + far)
        linear_across = after(linear_across, latest[-1])
        arrived = spread_near({0: linear_across})
        linear_pieces.update({half + place: arrived[place] for place in near})
        linear(2, near)
        for step in chunks:
            linear(step, far)

        out = jnp.zeros((shard_rows, mixed_width * n_batch), jnp.bfloat16)
        for group in range(2):
            for step in chunks:
                summed = lax.psum_scatter(
                    partial[step, group], "col", scatter_dimension=0, tiled=True
                )
                first = ((batch // half) ^ group) * half * mixed_width
                bias = lax.dynamic_slice_in_dim(linear_bias, first, half * mixed_width)
                out = lax.dynamic_update_slice(
                    out, (added(summed) + bias).astype(jnp.bfloat16), (starts[step], first)
                )
        return out

    return on_device


def solution(mesh):
    return jax.shard_map(
        build(mesh),
        mesh=mesh,
        in_specs=(
            P(("col", "batch"), "row"),
            P("row", ("col", "batch")),
            P("col"),
            P(),
            P("col", ("row", "batch")),
            P("row"),
        ),
        out_specs=P(("col", "batch"), "row"),
        check_vma=False,
    )
```

```python
import functools

import jax
import jax.numpy as jnp
from jax import lax
from jax.experimental import pallas as pl
from jax.experimental.pallas import tpu as pltpu
from jax.sharding import PartitionSpec as P

SHARES = (4, 4)
VMEM_BYTES = 48 * 2**20


def far_and_near(size, bit):
    return [(place, place ^ bit) for place in range(size)]


def cross_kernel(steps, meta, samples, *refs):
    weights, out, total = refs[:-2], refs[-2], refs[-1]
    step = lax.rem(pl.program_id(0), steps)
    piece = pl.program_id(0) // steps

    @pl.when(step == 0)
    def _():
        total[...] = jnp.zeros_like(total)

    for place, weight in enumerate(weights):

        @pl.when((piece == place) & (step < meta[place * (steps + 1)]))
        def _():
            total[...] += jnp.dot(samples[...], weight[...], preferred_element_type=jnp.float32)

    @pl.when(step == steps - 1)
    def _():
        out[...] = total[...].astype(out.dtype)


def cross_product(meta, samples, weights, block):
    rows, depth = samples.shape
    columns = weights[0].shape[1]
    steps = depth // block

    def listed(place, step, meta):
        return meta[place * (steps + 1) + 1 + step]

    def weight_spec(place):
        return pl.BlockSpec(
            (block, columns),
            lambda i, meta: (listed(place, jnp.clip(i - place * steps, 0, steps - 1), meta), 0),
        )

    return pl.pallas_call(
        functools.partial(cross_kernel, steps),
        out_shape=jax.ShapeDtypeStruct((rows, columns * len(weights)), jnp.bfloat16),
        grid_spec=pltpu.PrefetchScalarGridSpec(
            num_scalar_prefetch=1,
            grid=(len(weights) * steps,),
            in_specs=[
                pl.BlockSpec(
                    (rows, block), lambda i, meta: (0, listed(i // steps, lax.rem(i, steps), meta))
                ),
                *(weight_spec(place) for place in range(len(weights))),
            ],
            out_specs=pl.BlockSpec((rows, columns), lambda i, meta: (0, i // steps)),
            scratch_shapes=[pltpu.VMEM((rows, columns), jnp.float32)],
        ),
        compiler_params=pltpu.CompilerParams(vmem_limit_bytes=VMEM_BYTES),
        cost_estimate=pl.CostEstimate(
            flops=rows * depth * columns * len(weights),
            bytes_accessed=(rows * depth + depth * columns + 2 * rows * columns) * len(weights),
            transcendentals=0,
        ),
    )(meta, samples, *weights)


def linear_kernel(groups, parts, per_piece, meta, *refs):
    mine, theirs = refs[:groups], refs[groups : 2 * groups]
    weights, out, joined, sems = refs[2 * groups : -3], refs[-3], refs[-2], refs[-1]
    step = pl.program_id(0)
    pieces = sems.shape[0]
    width = joined.shape[1] // pieces
    in_group = pieces // groups

    @pl.when(step == 0)
    def _():
        def copy(sources, apart):
            columns = pl.ds(pl.multiple_of(meta[1 + apart] * width, width), width)
            source = sources[apart // in_group]
            first = apart % in_group * width
            return pltpu.make_async_copy(
                source.at[:, pl.ds(first, width)], joined.at[:, columns], sems.at[apart]
            )

        @pl.when(meta[0] == 1)
        def _():
            for apart in range(pieces):
                copy(mine, apart).start()
            for apart in range(pieces):
                copy(mine, apart).wait()

        @pl.when(meta[0] == 0)
        def _():
            for apart in range(pieces):
                copy(theirs, apart).start()
            for apart in range(pieces):
                copy(theirs, apart).wait()

    depth = joined.shape[1] // parts
    for place in range(len(weights) // parts):

        @pl.when(step // per_piece == place)
        def _():
            total = jnp.dot(
                joined[:, :depth], weights[place * parts][...], preferred_element_type=jnp.float32
            )
            for part in range(1, parts):
                total += jnp.dot(
                    joined[:, part * depth : (part + 1) * depth],
                    weights[place * parts + part][...],
                    preferred_element_type=jnp.float32,
                )
            out[...] = total.astype(out.dtype)


def linear_product(meta, pieces, mine, theirs, weights):
    groups, parts = len(mine), len(weights[0])
    rows = mine[0].shape[0]
    depth, columns = weights[0][0].shape
    whole_depth = depth * parts
    tile = min(columns, 512)
    per_piece = columns // tile
    anywhere = pl.BlockSpec(memory_space=pl.ANY)

    def weight_spec(place):
        return pl.BlockSpec(
            (depth, tile),
            lambda i, meta: (0, jnp.clip(i - place * per_piece, 0, per_piece - 1)),
        )

    def out_index(i, meta):
        return 0, meta[1 + pieces + i // per_piece] * per_piece + i % per_piece

    return pl.pallas_call(
        functools.partial(linear_kernel, groups, parts, per_piece),
        out_shape=jax.ShapeDtypeStruct((rows, columns * len(weights)), jnp.bfloat16),
        grid_spec=pltpu.PrefetchScalarGridSpec(
            num_scalar_prefetch=1,
            grid=(per_piece * len(weights),),
            in_specs=[anywhere] * (2 * groups)
            + [weight_spec(place) for place in range(len(weights)) for _ in range(parts)],
            out_specs=pl.BlockSpec((rows, tile), out_index),
            scratch_shapes=[
                pltpu.VMEM((rows, whole_depth), jnp.bfloat16),
                pltpu.SemaphoreType.DMA((pieces,)),
            ],
        ),
        compiler_params=pltpu.CompilerParams(vmem_limit_bytes=VMEM_BYTES),
        cost_estimate=pl.CostEstimate(
            flops=2 * rows * whole_depth * columns * len(weights),
            bytes_accessed=2 * rows * whole_depth
            + 2 * (whole_depth + rows) * columns * len(weights),
            transcendentals=0,
        ),
    )(meta, *mine, *theirs, *(part for weight in weights for part in weight))


def after(value, *others):
    return lax.optimization_barrier((value, *others))[0]


def added(*terms):
    return sum(term.astype(jnp.float32) for term in terms)


def finish_kernel(meta, own, came, samples, bias, out):
    base = samples[...].astype(jnp.float32)
    hidden = own[...].astype(jnp.float32) + came[...].astype(jnp.float32)
    out[...] = (base * (hidden + bias[...]) + base).astype(out.dtype)


def finish_cross(meta, own, came, samples, bias, pieces):
    rows, columns = own.shape[0], own.shape[1] // pieces
    part = pl.BlockSpec((rows, columns), lambda i, meta: (0, i))
    return pl.pallas_call(
        finish_kernel,
        out_shape=jax.ShapeDtypeStruct(own.shape, jnp.bfloat16),
        grid_spec=pltpu.PrefetchScalarGridSpec(
            num_scalar_prefetch=1,
            grid=(pieces,),
            in_specs=[
                part,
                part,
                pl.BlockSpec((rows, columns), lambda i, meta: (0, meta[2 * i])),
                pl.BlockSpec((1, columns), lambda i, meta: (0, meta[2 * i + 1])),
            ],
            out_specs=part,
        ),
        compiler_params=pltpu.CompilerParams(vmem_limit_bytes=VMEM_BYTES),
        cost_estimate=pl.CostEstimate(
            flops=4 * rows * columns * pieces,
            bytes_accessed=8 * rows * columns * pieces,
            transcendentals=0,
        ),
    )(meta, own, came, samples, bias)


class LineSum:
    def __init__(self, partial, place, size):
        self.partial, self.place, self.size = partial, place, size
        self.rows = partial.shape[0] // size
        self.begun = []
        if size == 4:
            inward = [(0, 1), (3, 2)]
            self.begun = [lax.ppermute(self.part(i), "col", inward) for i in (3, 2, 1)]

    def part(self, if_lower):
        upper = self.place >= self.size // 2
        first = jnp.where(upper, self.size - 1 - if_lower, if_lower) * self.rows
        return lax.dynamic_slice_in_dim(self.partial, first, self.rows, 0)

    def end(self):
        if self.size != 4:
            summed = lax.psum_scatter(self.partial, "col", scatter_dimension=0, tiled=True)
            return summed.astype(jnp.float32)
        across, outward = [(1, 2), (2, 1)], [(1, 0), (2, 3)]
        from_3, from_2, from_1 = self.begun
        over_3 = lax.ppermute(added(self.part(3), from_3).astype(jnp.bfloat16), "col", across)
        over_2 = lax.ppermute(added(self.part(2), from_2).astype(jnp.bfloat16), "col", across)
        out_0 = lax.ppermute(added(self.part(0), over_3).astype(jnp.bfloat16), "col", outward)
        own = lax.dynamic_slice_in_dim(self.partial, self.place * self.rows, self.rows, 0)
        is_end = (self.place == 0) | (self.place == self.size - 1)
        return added(own) + jnp.where(is_end, added(out_0), added(from_1, over_2))


def build(mesh):
    n_row, n_col, n_batch = (mesh.shape[name] for name in ("row", "col", "batch"))

    def on_device(features, cross_weight, cross_bias, pattern, linear_weight, linear_bias):
        input_width, piece_width = cross_weight.shape
        width = input_width * n_row
        output_width = piece_width * n_batch
        mixed_width = linear_weight.shape[1]
        block = width // pattern.shape[0]
        in_blocks = input_width // block
        row, col, batch = (lax.axis_index(name) for name in ("row", "col", "batch"))
        half = n_batch // 2

        def to_batch(shard, bit):
            return lax.ppermute(shard, "batch", far_and_near(n_batch, bit))

        def spread_near(pieces):
            bit = half // 2
            while bit:
                for apart in list(pieces):
                    pieces[apart | bit] = to_batch(pieces[apart], bit)
                bit //= 2
            return pieces

        cross_across = to_batch(cross_weight, half)
        parts = jnp.split(linear_weight, 2, axis=0)
        linear_across = [to_batch(part, half) for part in parts]
        cross_pieces = spread_near({0: cross_weight})
        linear_pieces = {
            place: [piece] for place, piece in spread_near({0: linear_weight}).items()
        }

        shard_rows = features.shape[0]
        starts = [shard_rows * sum(SHARES[:i]) // sum(SHARES) for i in range(len(SHARES) + 1)]
        shards = [features[first:last] for first, last in zip(starts, starts[1:])]
        gathered = [lax.all_gather(shard, "col", axis=0, tiled=True) for shard in shards]

        def kept_list(apart):
            out_block = (col * n_batch + (batch ^ apart)) * piece_width // block
            kept = lax.dynamic_slice(pattern, (out_block, row * in_blocks), (1, in_blocks))[0]
            number = jnp.sum(kept)
            rank = jnp.cumsum(kept) - 1
            slots = jnp.minimum(jnp.arange(in_blocks), jnp.maximum(number - 1, 0))
            match = (rank[None, :] == slots[:, None]) & (kept[None, :] == 1)
            listed = jnp.sum(jnp.where(match, jnp.arange(in_blocks)[None, :], 0), axis=1)
            return jnp.concatenate([number[None], listed]).astype(jnp.int32)

        kept_lists = [kept_list(apart) for apart in range(n_batch)]

        def owner_of(column):
            return column * output_width // input_width

        is_owner = row == col * output_width // input_width
        turns = [
            [
                ((owner_of(c) + turn) % n_row * n_col + c, owner_of(c) * n_col + c)
                for c in range(n_col)
            ]
            for turn in range(1, n_row)
        ]
        first_base = jnp.where(is_owner, col * output_width - row * input_width, 0)

        chunks = range(len(SHARES))
        bias_row = cross_bias[None, :]
        near, far = 0, 1
        in_group = [list(range(half)), list(range(half, n_batch))]
        products, came, mine, theirs, partial = {}, {}, {}, {}, {}
        latest = []

        def in_turn(meta, *others):
            return after(meta.astype(jnp.int32), *latest[-1:], *others)

        def multiply(step, group, *others):
            lists = jnp.concatenate([kept_lists[apart] for apart in in_group[group]])
            product = cross_product(
                in_turn(lists, *others),
                gathered[step],
                [cross_pieces[apart] for apart in in_group[group]],
                block,
            )
            latest.append(product)
            sent = [lax.ppermute(product, ("row", "col"), pairs) for pairs in turns]
            products[step, group], came[step, group] = product, sum(sent[1:], sent[0])

        def finish(step, group, *others):
            places = []
            for apart in in_group[group]:
                places += [first_base // piece_width + (batch ^ apart), batch ^ apart]
            crossed = finish_cross(
                in_turn(jnp.stack(places), *others),
                products[step, group],
                came[step, group],
                gathered[step],
                bias_row,
                half,
            )
            latest.append(crossed)
            back = [
                lax.ppermute(crossed, ("row", "col"), [(to, source) for source, to in pairs])
                for pairs in turns
            ]
            mine[step, group], theirs[step, group] = crossed, sum(back[1:], back[0])

        meta = jnp.stack(
            [is_owner.astype(jnp.int32)]
            + [batch ^ place for place in range(n_batch)]
            + [(batch ^ place) % half for place in range(half)]
        )

        def linear(step, group, *others):
            product = linear_product(
                in_turn(meta, *others),
                n_batch,
                [mine[step, g] for g in (near, far)],
                [theirs[step, g] for g in (near, far)],
                [linear_pieces[apart] for apart in in_group[group]],
            )
            latest.append(product)
            partial[step, group] = product

        def spread_far_cross(*others):
            arrived = spread_near({0: after(cross_across, *others)})
            cross_pieces.update({half + place: arrived[place] for place in range(half)})

        def spread_far_linear():
            arrived = [spread_near({0: part}) for part in linear_across]
            for place in range(half):
                linear_pieces[half + place] = [part[place] for part in arrived]

        begun = {}
        multiply(0, near)
        spread_far_cross(latest[-1])
        multiply(0, far)
        finish(0, near)
        finish(0, far)
        linear(0, near, gathered[1])
        summed_first = lax.psum_scatter(
            partial[0, near], "col", scatter_dimension=0, tiled=True
        )
        multiply(1, near, linear_across[0])
        multiply(1, far)
        linear_across[1] = after(linear_across[1], latest[-1])
        spread_far_linear()
        finish(1, near)
        linear(0, far)
        begun[0] = LineSum(partial[0, far], col, n_col)
        finish(1, far, summed_first, *begun[0].begun[:1])
        linear(1, far)
        begun[1] = LineSum(partial[1, far], col, n_col)
        linear(1, near)

        out = jnp.zeros((shard_rows, mixed_width * n_batch), jnp.bfloat16)
        for step, group in ((0, near), (0, far), (1, far), (1, near)):
            if group == far:
                summed = begun[step].end()
            elif step == 0:
                summed = summed_first
            else:
                summed = lax.psum_scatter(
                    partial[step, group], "col", scatter_dimension=0, tiled=True
                )
            first = ((batch // half) ^ group) * half * mixed_width
            bias = lax.dynamic_slice_in_dim(linear_bias, first, half * mixed_width)
            out = lax.dynamic_update_slice(
                out, (added(summed) + bias).astype(jnp.bfloat16), (starts[step], first)
            )
        return out

    return on_device


def solution(mesh):
    return jax.shard_map(
        build(mesh),
        mesh=mesh,
        in_specs=(
            P(("col", "batch"), "row"),
            P("row", ("col", "batch")),
            P("col"),
            P(),
            P("col", ("row", "batch")),
            P("row"),
        ),
        out_specs=P(("col", "batch"), "row"),
        check_vma=False,
    )
```

```python
import functools

import jax
import jax.numpy as jnp
from jax import lax
from jax.experimental import pallas as pl
from jax.experimental.pallas import tpu as pltpu
from jax.sharding import PartitionSpec as P

SHARES = (4, 4)
VMEM_BYTES = 48 * 2**20


def far_and_near(size, bit):
    return [(place, place ^ bit) for place in range(size)]


def cross_kernel(steps, meta, samples, *refs):
    weights, out, total = refs[:-2], refs[-2], refs[-1]
    step = lax.rem(pl.program_id(0), steps)
    piece = pl.program_id(0) // steps

    @pl.when(step == 0)
    def _():
        total[...] = jnp.zeros_like(total)

    for place, weight in enumerate(weights):

        @pl.when((piece == place) & (step < meta[place * (steps + 1)]))
        def _():
            total[...] += jnp.dot(samples[...], weight[...], preferred_element_type=jnp.float32)

    @pl.when(step == steps - 1)
    def _():
        out[...] = total[...].astype(out.dtype)


def cross_product(meta, samples, weights, block):
    rows, depth = samples.shape
    columns = weights[0].shape[1]
    steps = depth // block

    def listed(place, step, meta):
        return meta[place * (steps + 1) + 1 + step]

    def weight_spec(place):
        return pl.BlockSpec(
            (block, columns),
            lambda i, meta: (listed(place, jnp.clip(i - place * steps, 0, steps - 1), meta), 0),
        )

    return pl.pallas_call(
        functools.partial(cross_kernel, steps),
        out_shape=jax.ShapeDtypeStruct((rows, columns * len(weights)), jnp.bfloat16),
        grid_spec=pltpu.PrefetchScalarGridSpec(
            num_scalar_prefetch=1,
            grid=(len(weights) * steps,),
            in_specs=[
                pl.BlockSpec(
                    (rows, block), lambda i, meta: (0, listed(i // steps, lax.rem(i, steps), meta))
                ),
                *(weight_spec(place) for place in range(len(weights))),
            ],
            out_specs=pl.BlockSpec((rows, columns), lambda i, meta: (0, i // steps)),
            scratch_shapes=[pltpu.VMEM((rows, columns), jnp.float32)],
        ),
        compiler_params=pltpu.CompilerParams(vmem_limit_bytes=VMEM_BYTES),
        cost_estimate=pl.CostEstimate(
            flops=rows * depth * columns * len(weights),
            bytes_accessed=(rows * depth + depth * columns + 2 * rows * columns) * len(weights),
            transcendentals=0,
        ),
    )(meta, samples, *weights)


def linear_kernel(groups, parts, per_piece, meta, *refs):
    mine, theirs = refs[:groups], refs[groups : 2 * groups]
    weights, out, joined, sems = refs[2 * groups : -3], refs[-3], refs[-2], refs[-1]
    step = pl.program_id(0)
    pieces = sems.shape[0]
    width = joined.shape[1] // pieces
    in_group = pieces // groups

    @pl.when(step == 0)
    def _():
        def copy(sources, apart):
            columns = pl.ds(pl.multiple_of(meta[1 + apart] * width, width), width)
            source = sources[apart // in_group]
            first = apart % in_group * width
            return pltpu.make_async_copy(
                source.at[:, pl.ds(first, width)], joined.at[:, columns], sems.at[apart]
            )

        @pl.when(meta[0] == 1)
        def _():
            for apart in range(pieces):
                copy(mine, apart).start()
            for apart in range(pieces):
                copy(mine, apart).wait()

        @pl.when(meta[0] == 0)
        def _():
            for apart in range(pieces):
                copy(theirs, apart).start()
            for apart in range(pieces):
                copy(theirs, apart).wait()

    depth = joined.shape[1] // parts
    for place in range(len(weights) // parts):

        @pl.when(step // per_piece == place)
        def _():
            total = jnp.dot(
                joined[:, :depth], weights[place * parts][...], preferred_element_type=jnp.float32
            )
            for part in range(1, parts):
                total += jnp.dot(
                    joined[:, part * depth : (part + 1) * depth],
                    weights[place * parts + part][...],
                    preferred_element_type=jnp.float32,
                )
            out[...] = total.astype(out.dtype)


def linear_product(meta, pieces, mine, theirs, weights):
    groups, parts = len(mine), len(weights[0])
    rows = mine[0].shape[0]
    depth, columns = weights[0][0].shape
    whole_depth = depth * parts
    tile = min(columns, 512)
    per_piece = columns // tile
    anywhere = pl.BlockSpec(memory_space=pl.ANY)

    def weight_spec(place):
        return pl.BlockSpec(
            (depth, tile),
            lambda i, meta: (0, jnp.clip(i - place * per_piece, 0, per_piece - 1)),
        )

    def out_index(i, meta):
        return 0, meta[1 + pieces + i // per_piece] * per_piece + i % per_piece

    return pl.pallas_call(
        functools.partial(linear_kernel, groups, parts, per_piece),
        out_shape=jax.ShapeDtypeStruct((rows, columns * len(weights)), jnp.bfloat16),
        grid_spec=pltpu.PrefetchScalarGridSpec(
            num_scalar_prefetch=1,
            grid=(per_piece * len(weights),),
            in_specs=[anywhere] * (2 * groups)
            + [weight_spec(place) for place in range(len(weights)) for _ in range(parts)],
            out_specs=pl.BlockSpec((rows, tile), out_index),
            scratch_shapes=[
                pltpu.VMEM((rows, whole_depth), jnp.bfloat16),
                pltpu.SemaphoreType.DMA((pieces,)),
            ],
        ),
        compiler_params=pltpu.CompilerParams(vmem_limit_bytes=VMEM_BYTES),
        cost_estimate=pl.CostEstimate(
            flops=2 * rows * whole_depth * columns * len(weights),
            bytes_accessed=2 * rows * whole_depth
            + 2 * (whole_depth + rows) * columns * len(weights),
            transcendentals=0,
        ),
    )(meta, *mine, *theirs, *(part for weight in weights for part in weight))


def after(value, *others):
    return lax.optimization_barrier((value, *others))[0]


def added(*terms):
    return sum(term.astype(jnp.float32) for term in terms)


def finish_kernel(meta, own, came, samples, bias, out):
    base = samples[...].astype(jnp.float32)
    hidden = own[...].astype(jnp.float32) + came[...].astype(jnp.float32)
    out[...] = (base * (hidden + bias[...]) + base).astype(out.dtype)


def finish_cross(meta, own, came, samples, bias, pieces):
    rows, columns = own.shape[0], own.shape[1] // pieces
    part = pl.BlockSpec((rows, columns), lambda i, meta: (0, i))
    return pl.pallas_call(
        finish_kernel,
        out_shape=jax.ShapeDtypeStruct(own.shape, jnp.bfloat16),
        grid_spec=pltpu.PrefetchScalarGridSpec(
            num_scalar_prefetch=1,
            grid=(pieces,),
            in_specs=[
                part,
                part,
                pl.BlockSpec((rows, columns), lambda i, meta: (0, meta[2 * i])),
                pl.BlockSpec((1, columns), lambda i, meta: (0, meta[2 * i + 1])),
            ],
            out_specs=part,
        ),
        compiler_params=pltpu.CompilerParams(vmem_limit_bytes=VMEM_BYTES),
        cost_estimate=pl.CostEstimate(
            flops=4 * rows * columns * pieces,
            bytes_accessed=8 * rows * columns * pieces,
            transcendentals=0,
        ),
    )(meta, own, came, samples, bias)


class LineSum:
    def __init__(self, partial, place, size):
        self.partial, self.place, self.size = partial, place, size
        self.rows = partial.shape[0] // size
        self.begun = []
        if size == 4:
            inward = [(0, 1), (3, 2)]
            self.begun = [lax.ppermute(self.part(i), "col", inward) for i in (3, 2, 1)]

    def part(self, if_lower):
        upper = self.place >= self.size // 2
        first = jnp.where(upper, self.size - 1 - if_lower, if_lower) * self.rows
        return lax.dynamic_slice_in_dim(self.partial, first, self.rows, 0)

    def end(self):
        if self.size != 4:
            summed = lax.psum_scatter(self.partial, "col", scatter_dimension=0, tiled=True)
            return summed.astype(jnp.float32)
        across, outward = [(1, 2), (2, 1)], [(1, 0), (2, 3)]
        from_3, from_2, from_1 = self.begun
        over_3 = lax.ppermute(added(self.part(3), from_3).astype(jnp.bfloat16), "col", across)
        over_2 = lax.ppermute(added(self.part(2), from_2).astype(jnp.bfloat16), "col", across)
        out_0 = lax.ppermute(added(self.part(0), over_3).astype(jnp.bfloat16), "col", outward)
        own = lax.dynamic_slice_in_dim(self.partial, self.place * self.rows, self.rows, 0)
        is_end = (self.place == 0) | (self.place == self.size - 1)
        return added(own) + jnp.where(is_end, added(out_0), added(from_1, over_2))


class LineGather:
    def __init__(self, shard, place):
        self.shard, self.place = shard, place
        self.beside = lax.ppermute(shard, "col", [(0, 1), (1, 0), (2, 3), (3, 2)])
        self.over = lax.ppermute(shard, "col", [(1, 2), (2, 1)])

    def relay(self):
        outward = [(1, 0), (2, 3)]
        self.out = lax.ppermute(self.over, "col", outward)
        self.over_beside = lax.ppermute(self.beside, "col", [(1, 2), (2, 1)])
        self.out_beside = lax.ppermute(self.over_beside, "col", outward)

    def whole(self):
        place, shard = self.place, self.shard
        is_end = (place == 0) | (place == 3)
        lower = place < 2
        rows = shard.shape[0]
        whole = jnp.zeros((4 * rows, shard.shape[1]), shard.dtype)
        for part, at in (
            (shard, place),
            (self.beside, place ^ 1),
            (jnp.where(is_end, self.out, self.over), jnp.where(lower, 2, 1)),
            (jnp.where(is_end, self.out_beside, self.over_beside), jnp.where(lower, 3, 0)),
        ):
            whole = lax.dynamic_update_slice_in_dim(whole, part, at * rows, 0)
        return whole


class PlainGather:
    def __init__(self, shard, place):
        self.shard = self.beside = self.over = self.out = self.over_beside = self.out_beside = shard

    def relay(self):
        pass

    def whole(self):
        return lax.all_gather(self.shard, "col", axis=0, tiled=True)


def build(mesh):
    n_row, n_col, n_batch = (mesh.shape[name] for name in ("row", "col", "batch"))

    def on_device(features, cross_weight, cross_bias, pattern, linear_weight, linear_bias):
        input_width, piece_width = cross_weight.shape
        width = input_width * n_row
        output_width = piece_width * n_batch
        mixed_width = linear_weight.shape[1]
        block = width // pattern.shape[0]
        in_blocks = input_width // block
        row, col, batch = (lax.axis_index(name) for name in ("row", "col", "batch"))
        half = n_batch // 2

        def to_batch(shard, bit):
            return lax.ppermute(shard, "batch", far_and_near(n_batch, bit))

        def spread_near(pieces):
            bit = half // 2
            while bit:
                for apart in list(pieces):
                    pieces[apart | bit] = to_batch(pieces[apart], bit)
                bit //= 2
            return pieces

        cross_across = to_batch(cross_weight, half)
        parts = jnp.split(linear_weight, 2, axis=0)
        linear_across = [to_batch(part, half) for part in parts]
        linear_pieces = {
            place: [piece] for place, piece in spread_near({0: linear_weight}).items()
        }

        shard_rows = features.shape[0]
        starts = [shard_rows * sum(SHARES[:i]) // sum(SHARES) for i in range(len(SHARES) + 1)]
        shards = [features[first:last] for first, last in zip(starts, starts[1:])]
        gathers = [(LineGather if n_col == 4 else PlainGather)(shard, col) for shard in shards]
        for gather in gathers:
            gather.relay()
        gathered = [gather.whole() for gather in gathers]
        cross_pieces = spread_near({0: after(cross_weight, gathers[0].beside)})
        cross_pieces[0] = cross_weight

        def kept_list(apart):
            out_block = (col * n_batch + (batch ^ apart)) * piece_width // block
            kept = lax.dynamic_slice(pattern, (out_block, row * in_blocks), (1, in_blocks))[0]
            number = jnp.sum(kept)
            rank = jnp.cumsum(kept) - 1
            slots = jnp.minimum(jnp.arange(in_blocks), jnp.maximum(number - 1, 0))
            match = (rank[None, :] == slots[:, None]) & (kept[None, :] == 1)
            listed = jnp.sum(jnp.where(match, jnp.arange(in_blocks)[None, :], 0), axis=1)
            return jnp.concatenate([number[None], listed]).astype(jnp.int32)

        kept_lists = [kept_list(apart) for apart in range(n_batch)]

        def owner_of(column):
            return column * output_width // input_width

        is_owner = row == col * output_width // input_width
        turns = [
            [
                ((owner_of(c) + turn) % n_row * n_col + c, owner_of(c) * n_col + c)
                for c in range(n_col)
            ]
            for turn in range(1, n_row)
        ]
        first_base = jnp.where(is_owner, col * output_width - row * input_width, 0)

        chunks = range(len(SHARES))
        bias_row = cross_bias[None, :]
        near, far = 0, 1
        in_group = [list(range(half)), list(range(half, n_batch))]
        products, came, mine, theirs, partial = {}, {}, {}, {}, {}
        latest = []

        def in_turn(meta, *others):
            return after(meta.astype(jnp.int32), *latest[-1:], *others)

        def multiply(step, group, *others):
            lists = jnp.concatenate([kept_lists[apart] for apart in in_group[group]])
            product = cross_product(
                in_turn(lists, *others),
                gathered[step],
                [cross_pieces[apart] for apart in in_group[group]],
                block,
            )
            latest.append(product)
            sent = [lax.ppermute(product, ("row", "col"), pairs) for pairs in turns]
            products[step, group], came[step, group] = product, sum(sent[1:], sent[0])

        def finish(step, group, *others):
            places = []
            for apart in in_group[group]:
                places += [first_base // piece_width + (batch ^ apart), batch ^ apart]
            crossed = finish_cross(
                in_turn(jnp.stack(places), *others),
                products[step, group],
                came[step, group],
                gathered[step],
                bias_row,
                half,
            )
            latest.append(crossed)
            back = [
                lax.ppermute(crossed, ("row", "col"), [(to, source) for source, to in pairs])
                for pairs in turns
            ]
            mine[step, group], theirs[step, group] = crossed, sum(back[1:], back[0])

        meta = jnp.stack(
            [is_owner.astype(jnp.int32)]
            + [batch ^ place for place in range(n_batch)]
            + [(batch ^ place) % half for place in range(half)]
        )

        def linear(step, group, *others):
            product = linear_product(
                in_turn(meta, *others),
                n_batch,
                [mine[step, g] for g in (near, far)],
                [theirs[step, g] for g in (near, far)],
                [linear_pieces[apart] for apart in in_group[group]],
            )
            latest.append(product)
            partial[step, group] = product

        def spread_far_cross(*others):
            arrived = spread_near({0: after(cross_across, *others)})
            cross_pieces.update({half + place: arrived[place] for place in range(half)})

        def spread_far_linear():
            arrived = [spread_near({0: part}) for part in linear_across]
            for place in range(half):
                linear_pieces[half + place] = [part[place] for part in arrived]

        begun = {}
        later = gathers[1]
        multiply(0, near, later.beside, later.over, later.over_beside)
        spread_far_cross(latest[-1])
        finish(0, near, later.out)
        multiply(0, far)
        multiply(1, near, linear_across[0])
        finish(0, far)
        multiply(1, far)
        finish(1, near)
        linear(0, near)
        summed_first = lax.psum_scatter(
            partial[0, near], "col", scatter_dimension=0, tiled=True
        )
        finish(1, far)
        linear_across[1] = after(linear_across[1], latest[-1])
        spread_far_linear()
        linear(0, far)
        begun[0] = LineSum(partial[0, far], col, n_col)
        linear(1, near, *begun[0].begun[:1])
        linear(1, far, summed_first)
        begun[1] = LineSum(partial[1, far], col, n_col)

        out = jnp.zeros((shard_rows, mixed_width * n_batch), jnp.bfloat16)
        for step, group in ((0, near), (0, far), (1, far), (1, near)):
            if group == far:
                summed = begun[step].end()
            elif step == 0:
                summed = summed_first
            else:
                summed = lax.psum_scatter(
                    partial[step, group], "col", scatter_dimension=0, tiled=True
                )
            first = ((batch // half) ^ group) * half * mixed_width
            bias = lax.dynamic_slice_in_dim(linear_bias, first, half * mixed_width)
            out = lax.dynamic_update_slice(
                out, (added(summed) + bias).astype(jnp.bfloat16), (starts[step], first)
            )
        return out

    return on_device


def solution(mesh):
    return jax.shard_map(
        build(mesh),
        mesh=mesh,
        in_specs=(
            P(("col", "batch"), "row"),
            P("row", ("col", "batch")),
            P("col"),
            P(),
            P("col", ("row", "batch")),
            P("row"),
        ),
        out_specs=P(("col", "batch"), "row"),
        check_vma=False,
    )
```

```python
import functools

import jax
import jax.numpy as jnp
from jax import lax
from jax.experimental import pallas as pl
from jax.experimental.pallas import tpu as pltpu
from jax.sharding import PartitionSpec as P

SHARES = (4, 4)
VMEM_BYTES = 48 * 2**20


def far_and_near(size, bit):
    return [(place, place ^ bit) for place in range(size)]


def cross_kernel(steps, meta, samples, *refs):
    weights, out, total = refs[:-2], refs[-2], refs[-1]
    step = lax.rem(pl.program_id(0), steps)
    piece = pl.program_id(0) // steps

    @pl.when(step == 0)
    def _():
        total[...] = jnp.zeros_like(total)

    for place, weight in enumerate(weights):

        @pl.when((piece == place) & (step < meta[place * (steps + 1)]))
        def _():
            total[...] += jnp.dot(samples[...], weight[...], preferred_element_type=jnp.float32)

    @pl.when(step == steps - 1)
    def _():
        out[...] = total[...].astype(out.dtype)


def cross_product(meta, samples, weights, block):
    rows, depth = samples.shape
    columns = weights[0].shape[1]
    steps = depth // block

    def listed(place, step, meta):
        return meta[place * (steps + 1) + 1 + step]

    def weight_spec(place):
        return pl.BlockSpec(
            (block, columns),
            lambda i, meta: (listed(place, jnp.clip(i - place * steps, 0, steps - 1), meta), 0),
        )

    return pl.pallas_call(
        functools.partial(cross_kernel, steps),
        out_shape=jax.ShapeDtypeStruct((rows, columns * len(weights)), jnp.bfloat16),
        grid_spec=pltpu.PrefetchScalarGridSpec(
            num_scalar_prefetch=1,
            grid=(len(weights) * steps,),
            in_specs=[
                pl.BlockSpec(
                    (rows, block), lambda i, meta: (0, listed(i // steps, lax.rem(i, steps), meta))
                ),
                *(weight_spec(place) for place in range(len(weights))),
            ],
            out_specs=pl.BlockSpec((rows, columns), lambda i, meta: (0, i // steps)),
            scratch_shapes=[pltpu.VMEM((rows, columns), jnp.float32)],
        ),
        compiler_params=pltpu.CompilerParams(vmem_limit_bytes=VMEM_BYTES),
        cost_estimate=pl.CostEstimate(
            flops=rows * depth * columns * len(weights),
            bytes_accessed=(rows * depth + depth * columns + 2 * rows * columns) * len(weights),
            transcendentals=0,
        ),
    )(meta, samples, *weights)


def linear_kernel(groups, parts, per_piece, meta, *refs):
    mine, theirs = refs[:groups], refs[groups : 2 * groups]
    weights, out, joined, sems = refs[2 * groups : -3], refs[-3], refs[-2], refs[-1]
    step = pl.program_id(0)
    pieces = sems.shape[0]
    width = joined.shape[1] // pieces
    in_group = pieces // groups

    @pl.when(step == 0)
    def _():
        def copy(sources, apart):
            columns = pl.ds(pl.multiple_of(meta[1 + apart] * width, width), width)
            source = sources[apart // in_group]
            first = apart % in_group * width
            return pltpu.make_async_copy(
                source.at[:, pl.ds(first, width)], joined.at[:, columns], sems.at[apart]
            )

        @pl.when(meta[0] == 1)
        def _():
            for apart in range(pieces):
                copy(mine, apart).start()
            for apart in range(pieces):
                copy(mine, apart).wait()

        @pl.when(meta[0] == 0)
        def _():
            for apart in range(pieces):
                copy(theirs, apart).start()
            for apart in range(pieces):
                copy(theirs, apart).wait()

    depth = joined.shape[1] // parts
    for place in range(len(weights) // parts):

        @pl.when(step // per_piece == place)
        def _():
            total = jnp.dot(
                joined[:, :depth], weights[place * parts][...], preferred_element_type=jnp.float32
            )
            for part in range(1, parts):
                total += jnp.dot(
                    joined[:, part * depth : (part + 1) * depth],
                    weights[place * parts + part][...],
                    preferred_element_type=jnp.float32,
                )
            out[...] = total.astype(out.dtype)


def linear_product(meta, pieces, mine, theirs, weights):
    groups, parts = len(mine), len(weights[0])
    rows = mine[0].shape[0]
    depth, columns = weights[0][0].shape
    whole_depth = depth * parts
    tile = min(columns, 512)
    per_piece = columns // tile
    anywhere = pl.BlockSpec(memory_space=pl.ANY)

    def weight_spec(place):
        return pl.BlockSpec(
            (depth, tile),
            lambda i, meta: (0, jnp.clip(i - place * per_piece, 0, per_piece - 1)),
        )

    def out_index(i, meta):
        return 0, meta[1 + pieces + i // per_piece] * per_piece + i % per_piece

    return pl.pallas_call(
        functools.partial(linear_kernel, groups, parts, per_piece),
        out_shape=jax.ShapeDtypeStruct((rows, columns * len(weights)), jnp.bfloat16),
        grid_spec=pltpu.PrefetchScalarGridSpec(
            num_scalar_prefetch=1,
            grid=(per_piece * len(weights),),
            in_specs=[anywhere] * (2 * groups)
            + [weight_spec(place) for place in range(len(weights)) for _ in range(parts)],
            out_specs=pl.BlockSpec((rows, tile), out_index),
            scratch_shapes=[
                pltpu.VMEM((rows, whole_depth), jnp.bfloat16),
                pltpu.SemaphoreType.DMA((pieces,)),
            ],
        ),
        compiler_params=pltpu.CompilerParams(vmem_limit_bytes=VMEM_BYTES),
        cost_estimate=pl.CostEstimate(
            flops=2 * rows * whole_depth * columns * len(weights),
            bytes_accessed=2 * rows * whole_depth
            + 2 * (whole_depth + rows) * columns * len(weights),
            transcendentals=0,
        ),
    )(meta, *mine, *theirs, *(part for weight in weights for part in weight))


def after(value, *others):
    return lax.optimization_barrier((value, *others))[0]


def added(*terms):
    return sum(term.astype(jnp.float32) for term in terms)


def finish_kernel(meta, own, came, samples, bias, out):
    base = samples[...].astype(jnp.float32)
    hidden = own[...].astype(jnp.float32) + came[...].astype(jnp.float32)
    out[...] = (base * (hidden + bias[...]) + base).astype(out.dtype)


def finish_cross(meta, own, came, samples, bias, pieces):
    rows, columns = own.shape[0], own.shape[1] // pieces
    part = pl.BlockSpec((rows, columns), lambda i, meta: (0, i))
    return pl.pallas_call(
        finish_kernel,
        out_shape=jax.ShapeDtypeStruct(own.shape, jnp.bfloat16),
        grid_spec=pltpu.PrefetchScalarGridSpec(
            num_scalar_prefetch=1,
            grid=(pieces,),
            in_specs=[
                part,
                part,
                pl.BlockSpec((rows, columns), lambda i, meta: (0, meta[2 * i])),
                pl.BlockSpec((1, columns), lambda i, meta: (0, meta[2 * i + 1])),
            ],
            out_specs=part,
        ),
        compiler_params=pltpu.CompilerParams(vmem_limit_bytes=VMEM_BYTES),
        cost_estimate=pl.CostEstimate(
            flops=4 * rows * columns * pieces,
            bytes_accessed=8 * rows * columns * pieces,
            transcendentals=0,
        ),
    )(meta, own, came, samples, bias)


class LineSum:
    def __init__(self, partial, place, size):
        self.partial, self.place, self.size = partial, place, size
        self.rows = partial.shape[0] // size
        self.begun = []
        if size == 4:
            inward = [(0, 1), (3, 2)]
            self.begun = [lax.ppermute(self.part(i), "col", inward) for i in (3, 2, 1)]

    def part(self, if_lower):
        upper = self.place >= self.size // 2
        first = jnp.where(upper, self.size - 1 - if_lower, if_lower) * self.rows
        return lax.dynamic_slice_in_dim(self.partial, first, self.rows, 0)

    def middle(self):
        self.over = []
        if self.size == 4:
            self.over = [
                lax.ppermute(
                    added(self.part(i), came).astype(jnp.bfloat16), "col", [(1, 2), (2, 1)]
                )
                for i, came in zip((3, 2), self.begun)
            ]
        return self.over

    def end(self):
        if self.size != 4:
            summed = lax.psum_scatter(self.partial, "col", scatter_dimension=0, tiled=True)
            return summed.astype(jnp.float32)
        over_3, over_2 = self.over
        from_1 = self.begun[2]
        out_0 = lax.ppermute(
            added(self.part(0), over_3).astype(jnp.bfloat16), "col", [(1, 0), (2, 3)]
        )
        own = lax.dynamic_slice_in_dim(self.partial, self.place * self.rows, self.rows, 0)
        is_end = (self.place == 0) | (self.place == self.size - 1)
        return added(own) + jnp.where(is_end, added(out_0), added(from_1, over_2))


def build(mesh):
    n_row, n_col, n_batch = (mesh.shape[name] for name in ("row", "col", "batch"))

    def on_device(features, cross_weight, cross_bias, pattern, linear_weight, linear_bias):
        input_width, piece_width = cross_weight.shape
        width = input_width * n_row
        output_width = piece_width * n_batch
        mixed_width = linear_weight.shape[1]
        block = width // pattern.shape[0]
        in_blocks = input_width // block
        row, col, batch = (lax.axis_index(name) for name in ("row", "col", "batch"))
        half = n_batch // 2

        def to_batch(shard, bit):
            return lax.ppermute(shard, "batch", far_and_near(n_batch, bit))

        def spread_near(pieces):
            bit = half // 2
            while bit:
                for apart in list(pieces):
                    pieces[apart | bit] = to_batch(pieces[apart], bit)
                bit //= 2
            return pieces

        cross_across = to_batch(cross_weight, half)
        parts = jnp.split(linear_weight, 2, axis=0)
        linear_across = [to_batch(part, half) for part in parts]
        cross_pieces = spread_near({0: cross_weight})
        linear_pieces = {
            place: [piece] for place, piece in spread_near({0: linear_weight}).items()
        }

        shard_rows = features.shape[0]
        starts = [shard_rows * sum(SHARES[:i]) // sum(SHARES) for i in range(len(SHARES) + 1)]
        shards = [features[first:last] for first, last in zip(starts, starts[1:])]
        gathered = [lax.all_gather(shard, "col", axis=0, tiled=True) for shard in shards]

        def kept_list(apart):
            out_block = (col * n_batch + (batch ^ apart)) * piece_width // block
            kept = lax.dynamic_slice(pattern, (out_block, row * in_blocks), (1, in_blocks))[0]
            number = jnp.sum(kept)
            rank = jnp.cumsum(kept) - 1
            slots = jnp.minimum(jnp.arange(in_blocks), jnp.maximum(number - 1, 0))
            match = (rank[None, :] == slots[:, None]) & (kept[None, :] == 1)
            listed = jnp.sum(jnp.where(match, jnp.arange(in_blocks)[None, :], 0), axis=1)
            return jnp.concatenate([number[None], listed]).astype(jnp.int32)

        kept_lists = [kept_list(apart) for apart in range(n_batch)]

        def owner_of(column):
            return column * output_width // input_width

        is_owner = row == col * output_width // input_width
        turns = [
            [
                ((owner_of(c) + turn) % n_row * n_col + c, owner_of(c) * n_col + c)
                for c in range(n_col)
            ]
            for turn in range(1, n_row)
        ]
        first_base = jnp.where(is_owner, col * output_width - row * input_width, 0)

        chunks = range(len(SHARES))
        bias_row = cross_bias[None, :]
        near, far = 0, 1
        in_group = [list(range(half)), list(range(half, n_batch))]
        places = {}
        for group in (near, far):
            listed = []
            for apart in in_group[group]:
                listed += [first_base // piece_width + (batch ^ apart), batch ^ apart]
            places[group] = jnp.stack(listed)
        products, came, mine, theirs, partial = {}, {}, {}, {}, {}
        latest = []

        def in_turn(meta, *others):
            return after(meta.astype(jnp.int32), *latest[-1:], *others)

        def multiply(step, group, *others):
            lists = jnp.concatenate([kept_lists[apart] for apart in in_group[group]])
            product = cross_product(
                in_turn(lists, *others),
                gathered[step],
                [cross_pieces[apart] for apart in in_group[group]],
                block,
            )
            latest.append(product)
            sent = [lax.ppermute(product, ("row", "col"), pairs) for pairs in turns]
            products[step, group], came[step, group] = product, sum(sent[1:], sent[0])

        def finish(step, group, *others):
            crossed = finish_cross(
                in_turn(places[group], *others),
                products[step, group],
                came[step, group],
                gathered[step],
                bias_row,
                half,
            )
            latest.append(crossed)
            back = [
                lax.ppermute(crossed, ("row", "col"), [(to, source) for source, to in pairs])
                for pairs in turns
            ]
            mine[step, group], theirs[step, group] = crossed, sum(back[1:], back[0])

        meta = jnp.stack(
            [is_owner.astype(jnp.int32)]
            + [batch ^ place for place in range(n_batch)]
            + [(batch ^ place) % half for place in range(half)]
        )

        def linear(step, group, *others):
            product = linear_product(
                in_turn(meta, *others),
                n_batch,
                [mine[step, g] for g in (near, far)],
                [theirs[step, g] for g in (near, far)],
                [linear_pieces[apart] for apart in in_group[group]],
            )
            latest.append(product)
            partial[step, group] = product

        def spread_far_cross(*others):
            arrived = spread_near({0: after(cross_across, *others)})
            cross_pieces.update({half + place: arrived[place] for place in range(half)})

        def spread_far_linear():
            arrived = [spread_near({0: part}) for part in linear_across]
            for place in range(half):
                linear_pieces[half + place] = [part[place] for part in arrived]

        begun = {}
        multiply(0, near, meta, *kept_lists, *places.values())
        spread_far_cross(latest[-1])
        multiply(0, far)
        finish(0, near)
        finish(0, far)
        multiply(1, near, linear_across[0])
        multiply(1, far)
        linear(0, near)
        summed_first = lax.psum_scatter(
            partial[0, near], "col", scatter_dimension=0, tiled=True
        )
        finish(1, near)
        finish(1, far)
        linear_across[1] = after(linear_across[1], latest[-1])
        spread_far_linear()
        linear(0, far, summed_first, theirs[1, near], theirs[1, far])
        begun[0] = LineSum(partial[0, far], col, n_col)
        linear(1, near)
        linear(1, far, *begun[0].middle()[:1])
        begun[1] = LineSum(partial[1, far], col, n_col)
        begun[1].middle()

        out = jnp.zeros((shard_rows, mixed_width * n_batch), jnp.bfloat16)
        for step, group in ((0, near), (0, far), (1, far), (1, near)):
            if group == far:
                summed = begun[step].end()
            elif step == 0:
                summed = summed_first
            else:
                summed = lax.psum_scatter(
                    partial[step, group], "col", scatter_dimension=0, tiled=True
                )
            first = ((batch // half) ^ group) * half * mixed_width
            bias = lax.dynamic_slice_in_dim(linear_bias, first, half * mixed_width)
            out = lax.dynamic_update_slice(
                out, (added(summed) + bias).astype(jnp.bfloat16), (starts[step], first)
            )
        return out

    return on_device


def solution(mesh):
    return jax.shard_map(
        build(mesh),
        mesh=mesh,
        in_specs=(
            P(("col", "batch"), "row"),
            P("row", ("col", "batch")),
            P("col"),
            P(),
            P("col", ("row", "batch")),
            P("row"),
        ),
        out_specs=P(("col", "batch"), "row"),
        check_vma=False,
    )
```

```python
import functools

import jax
import jax.numpy as jnp
from jax import lax
from jax.experimental import pallas as pl
from jax.experimental.pallas import tpu as pltpu
from jax.sharding import PartitionSpec as P

SHARES = (4, 4)
VMEM_BYTES = 48 * 2**20


def far_and_near(size, bit):
    return [(place, place ^ bit) for place in range(size)]


def cross_kernel(steps, meta, samples, *refs):
    weights, out, total = refs[:-2], refs[-2], refs[-1]
    step = lax.rem(pl.program_id(0), steps)
    piece = pl.program_id(0) // steps

    @pl.when(step == 0)
    def _():
        total[...] = jnp.zeros_like(total)

    for place, weight in enumerate(weights):

        @pl.when((piece == place) & (step < meta[place * (steps + 1)]))
        def _():
            total[...] += jnp.dot(samples[...], weight[...], preferred_element_type=jnp.float32)

    @pl.when(step == steps - 1)
    def _():
        out[...] = total[...].astype(out.dtype)


def cross_product(meta, samples, weights, block):
    rows, depth = samples.shape
    columns = weights[0].shape[1]
    steps = depth // block

    def listed(place, step, meta):
        return meta[place * (steps + 1) + 1 + step]

    def weight_spec(place):
        return pl.BlockSpec(
            (block, columns),
            lambda i, meta: (listed(place, jnp.clip(i - place * steps, 0, steps - 1), meta), 0),
        )

    return pl.pallas_call(
        functools.partial(cross_kernel, steps),
        out_shape=jax.ShapeDtypeStruct((rows, columns * len(weights)), jnp.bfloat16),
        grid_spec=pltpu.PrefetchScalarGridSpec(
            num_scalar_prefetch=1,
            grid=(len(weights) * steps,),
            in_specs=[
                pl.BlockSpec(
                    (rows, block), lambda i, meta: (0, listed(i // steps, lax.rem(i, steps), meta))
                ),
                *(weight_spec(place) for place in range(len(weights))),
            ],
            out_specs=pl.BlockSpec((rows, columns), lambda i, meta: (0, i // steps)),
            scratch_shapes=[pltpu.VMEM((rows, columns), jnp.float32)],
        ),
        compiler_params=pltpu.CompilerParams(vmem_limit_bytes=VMEM_BYTES),
        cost_estimate=pl.CostEstimate(
            flops=rows * depth * columns * len(weights),
            bytes_accessed=(rows * depth + depth * columns + 2 * rows * columns) * len(weights),
            transcendentals=0,
        ),
    )(meta, samples, *weights)


def linear_kernel(groups, parts, per_piece, meta, *refs):
    mine, theirs = refs[:groups], refs[groups : 2 * groups]
    weights, out, joined, sems = refs[2 * groups : -3], refs[-3], refs[-2], refs[-1]
    step = pl.program_id(0)
    pieces = sems.shape[0]
    width = joined.shape[1] // pieces
    in_group = pieces // groups

    @pl.when(step == 0)
    def _():
        def copy(sources, apart):
            columns = pl.ds(pl.multiple_of(meta[1 + apart] * width, width), width)
            source = sources[apart // in_group]
            first = apart % in_group * width
            return pltpu.make_async_copy(
                source.at[:, pl.ds(first, width)], joined.at[:, columns], sems.at[apart]
            )

        @pl.when(meta[0] == 1)
        def _():
            for apart in range(pieces):
                copy(mine, apart).start()
            for apart in range(pieces):
                copy(mine, apart).wait()

        @pl.when(meta[0] == 0)
        def _():
            for apart in range(pieces):
                copy(theirs, apart).start()
            for apart in range(pieces):
                copy(theirs, apart).wait()

    depth = joined.shape[1] // parts
    for place in range(len(weights) // parts):

        @pl.when(step // per_piece == place)
        def _():
            total = jnp.dot(
                joined[:, :depth], weights[place * parts][...], preferred_element_type=jnp.float32
            )
            for part in range(1, parts):
                total += jnp.dot(
                    joined[:, part * depth : (part + 1) * depth],
                    weights[place * parts + part][...],
                    preferred_element_type=jnp.float32,
                )
            out[...] = total.astype(out.dtype)


def linear_product(meta, pieces, mine, theirs, weights):
    groups, parts = len(mine), len(weights[0])
    rows = mine[0].shape[0]
    depth, columns = weights[0][0].shape
    whole_depth = depth * parts
    tile = min(columns, 512)
    per_piece = columns // tile
    anywhere = pl.BlockSpec(memory_space=pl.ANY)

    def weight_spec(place):
        return pl.BlockSpec(
            (depth, tile),
            lambda i, meta: (0, jnp.clip(i - place * per_piece, 0, per_piece - 1)),
        )

    def out_index(i, meta):
        return 0, meta[1 + pieces + i // per_piece] * per_piece + i % per_piece

    return pl.pallas_call(
        functools.partial(linear_kernel, groups, parts, per_piece),
        out_shape=jax.ShapeDtypeStruct((rows, columns * len(weights)), jnp.bfloat16),
        grid_spec=pltpu.PrefetchScalarGridSpec(
            num_scalar_prefetch=1,
            grid=(per_piece * len(weights),),
            in_specs=[anywhere] * (2 * groups)
            + [weight_spec(place) for place in range(len(weights)) for _ in range(parts)],
            out_specs=pl.BlockSpec((rows, tile), out_index),
            scratch_shapes=[
                pltpu.VMEM((rows, whole_depth), jnp.bfloat16),
                pltpu.SemaphoreType.DMA((pieces,)),
            ],
        ),
        compiler_params=pltpu.CompilerParams(vmem_limit_bytes=VMEM_BYTES),
        cost_estimate=pl.CostEstimate(
            flops=2 * rows * whole_depth * columns * len(weights),
            bytes_accessed=2 * rows * whole_depth
            + 2 * (whole_depth + rows) * columns * len(weights),
            transcendentals=0,
        ),
    )(meta, *mine, *theirs, *(part for weight in weights for part in weight))


def after(value, *others):
    return lax.optimization_barrier((value, *others))[0]


def added(*terms):
    return sum(term.astype(jnp.float32) for term in terms)


def finish_kernel(meta, own, came, samples, bias, out):
    base = samples[...].astype(jnp.float32)
    hidden = own[...].astype(jnp.float32) + came[...].astype(jnp.float32)
    out[...] = (base * (hidden + bias[...]) + base).astype(out.dtype)


def finish_cross(meta, own, came, samples, bias, pieces):
    rows, columns = own.shape[0], own.shape[1] // pieces
    part = pl.BlockSpec((rows, columns), lambda i, meta: (0, i))
    return pl.pallas_call(
        finish_kernel,
        out_shape=jax.ShapeDtypeStruct(own.shape, jnp.bfloat16),
        grid_spec=pltpu.PrefetchScalarGridSpec(
            num_scalar_prefetch=1,
            grid=(pieces,),
            in_specs=[
                part,
                part,
                pl.BlockSpec((rows, columns), lambda i, meta: (0, meta[2 * i])),
                pl.BlockSpec((1, columns), lambda i, meta: (0, meta[2 * i + 1])),
            ],
            out_specs=part,
        ),
        compiler_params=pltpu.CompilerParams(vmem_limit_bytes=VMEM_BYTES),
        cost_estimate=pl.CostEstimate(
            flops=4 * rows * columns * pieces,
            bytes_accessed=8 * rows * columns * pieces,
            transcendentals=0,
        ),
    )(meta, own, came, samples, bias)


class LineSum:
    def __init__(self, partial, place, size):
        self.partial, self.place, self.size = partial, place, size
        self.rows = partial.shape[0] // size
        self.begun = []
        if size == 4:
            inward = [(0, 1), (3, 2)]
            self.begun = [lax.ppermute(self.part(i), "col", inward) for i in (3, 2, 1)]

    def part(self, if_lower):
        upper = self.place >= self.size // 2
        first = jnp.where(upper, self.size - 1 - if_lower, if_lower) * self.rows
        return lax.dynamic_slice_in_dim(self.partial, first, self.rows, 0)

    def middle(self):
        self.over = []
        if self.size == 4:
            self.over = [
                lax.ppermute(
                    added(self.part(i), came).astype(jnp.bfloat16), "col", [(1, 2), (2, 1)]
                )
                for i, came in zip((3, 2), self.begun)
            ]
        return self.over

    def end(self):
        if self.size != 4:
            summed = lax.psum_scatter(self.partial, "col", scatter_dimension=0, tiled=True)
            return summed.astype(jnp.float32)
        over_3, over_2 = self.over
        from_1 = self.begun[2]
        out_0 = lax.ppermute(
            added(self.part(0), over_3).astype(jnp.bfloat16), "col", [(1, 0), (2, 3)]
        )
        own = lax.dynamic_slice_in_dim(self.partial, self.place * self.rows, self.rows, 0)
        is_end = (self.place == 0) | (self.place == self.size - 1)
        return added(own) + jnp.where(is_end, added(out_0), added(from_1, over_2))


def build(mesh):
    n_row, n_col, n_batch = (mesh.shape[name] for name in ("row", "col", "batch"))

    def on_device(features, cross_weight, cross_bias, pattern, linear_weight, linear_bias):
        input_width, piece_width = cross_weight.shape
        width = input_width * n_row
        output_width = piece_width * n_batch
        mixed_width = linear_weight.shape[1]
        block = width // pattern.shape[0]
        in_blocks = input_width // block
        row, col, batch = (lax.axis_index(name) for name in ("row", "col", "batch"))
        half = n_batch // 2

        def to_batch(shard, bit):
            return lax.ppermute(shard, "batch", far_and_near(n_batch, bit))

        def spread_near(pieces):
            bit = half // 2
            while bit:
                for apart in list(pieces):
                    pieces[apart | bit] = to_batch(pieces[apart], bit)
                bit //= 2
            return pieces

        cross_across = to_batch(cross_weight, half)
        parts = jnp.split(linear_weight, 2, axis=0)
        linear_across = [to_batch(part, half) for part in parts]
        cross_pieces = spread_near({0: cross_weight})
        linear_pieces = {
            place: [piece] for place, piece in spread_near({0: linear_weight}).items()
        }

        shard_rows = features.shape[0]
        starts = [shard_rows * sum(SHARES[:i]) // sum(SHARES) for i in range(len(SHARES) + 1)]
        shards = [features[first:last] for first, last in zip(starts, starts[1:])]
        gathered = [lax.all_gather(shard, "col", axis=0, tiled=True) for shard in shards]

        def kept_list(apart):
            out_block = (col * n_batch + (batch ^ apart)) * piece_width // block
            kept = lax.dynamic_slice(pattern, (out_block, row * in_blocks), (1, in_blocks))[0]
            number = jnp.sum(kept)
            rank = jnp.cumsum(kept) - 1
            slots = jnp.minimum(jnp.arange(in_blocks), jnp.maximum(number - 1, 0))
            match = (rank[None, :] == slots[:, None]) & (kept[None, :] == 1)
            listed = jnp.sum(jnp.where(match, jnp.arange(in_blocks)[None, :], 0), axis=1)
            return jnp.concatenate([number[None], listed]).astype(jnp.int32)

        kept_lists = [kept_list(apart) for apart in range(n_batch)]

        def owner_of(column):
            return column * output_width // input_width

        is_owner = row == col * output_width // input_width
        turns = [
            [
                ((owner_of(c) + turn) % n_row * n_col + c, owner_of(c) * n_col + c)
                for c in range(n_col)
            ]
            for turn in range(1, n_row)
        ]
        first_base = jnp.where(is_owner, col * output_width - row * input_width, 0)

        chunks = range(len(SHARES))
        bias_row = cross_bias[None, :]
        near, far = 0, 1
        in_group = [list(range(half)), list(range(half, n_batch))]
        places = {}
        for group in (near, far):
            listed = []
            for apart in in_group[group]:
                listed += [first_base // piece_width + (batch ^ apart), batch ^ apart]
            places[group] = jnp.stack(listed)
        products, came, mine, theirs, partial = {}, {}, {}, {}, {}
        latest = []

        def in_turn(meta, *others):
            return after(meta.astype(jnp.int32), *latest[-1:], *others)

        def multiply(step, group, *others, send=True):
            lists = jnp.concatenate([kept_lists[apart] for apart in in_group[group]])
            product = cross_product(
                in_turn(lists, *others),
                gathered[step],
                [cross_pieces[apart] for apart in in_group[group]],
                block,
            )
            latest.append(product)
            products[step, group] = product
            if send:
                sent = [lax.ppermute(product, ("row", "col"), pairs) for pairs in turns]
                came[step, group] = sum(sent[1:], sent[0])

        def finish(step, group, *others, beside=None):
            crossed = finish_cross(
                in_turn(places[group], *others),
                products[step, group],
                came[step, group],
                gathered[step],
                bias_row,
                half,
            )
            latest.append(crossed)
            returns = [[(to, source) for source, to in pairs] for pairs in turns]
            sent = crossed
            if beside is not None:
                sent = jnp.where(is_owner, crossed, products[step, beside])
                returns = [back + pairs for back, pairs in zip(returns, turns)]
            back = [lax.ppermute(sent, ("row", "col"), pairs) for pairs in returns]
            mine[step, group], theirs[step, group] = crossed, sum(back[1:], back[0])
            if beside is not None:
                came[step, beside] = theirs[step, group]

        meta = jnp.stack(
            [is_owner.astype(jnp.int32)]
            + [batch ^ place for place in range(n_batch)]
            + [(batch ^ place) % half for place in range(half)]
        )

        def linear(step, group, *others):
            product = linear_product(
                in_turn(meta, *others),
                n_batch,
                [mine[step, g] for g in (near, far)],
                [theirs[step, g] for g in (near, far)],
                [linear_pieces[apart] for apart in in_group[group]],
            )
            latest.append(product)
            partial[step, group] = product

        def spread_far_cross(*others):
            arrived = spread_near({0: after(cross_across, *others)})
            cross_pieces.update({half + place: arrived[place] for place in range(half)})

        def spread_far_linear(across):
            arrived = [spread_near({0: part}) for part in across]
            for place in range(half):
                linear_pieces[half + place] = [part[place] for part in arrived]

        begun = {}
        multiply(0, near, meta, *kept_lists, *places.values())
        spread_far_cross(latest[-1])
        multiply(0, far)
        finish(0, near, *(linear_pieces[place][0] for place in range(half)))
        finish(0, far)
        multiply(1, near, linear_across[0])
        multiply(1, far, send=False)
        linear(0, near)
        summed_first = lax.psum_scatter(
            partial[0, near], "col", scatter_dimension=0, tiled=True
        )
        finish(1, near, beside=far)
        finish(1, far)
        linear_across = [after(part, latest[-1]) for part in linear_across]
        spread_far_linear(linear_across)
        linear(0, far, summed_first, theirs[1, far])
        begun[0] = LineSum(partial[0, far], col, n_col)
        linear(1, near)
        linear(1, far, *begun[0].middle()[:1])
        begun[1] = LineSum(partial[1, far], col, n_col)
        begun[1].middle()

        out = jnp.zeros((shard_rows, mixed_width * n_batch), jnp.bfloat16)
        for step, group in ((0, near), (0, far), (1, far), (1, near)):
            if group == far:
                summed = begun[step].end()
            elif step == 0:
                summed = summed_first
            else:
                summed = lax.psum_scatter(
                    partial[step, group], "col", scatter_dimension=0, tiled=True
                )
            first = ((batch // half) ^ group) * half * mixed_width
            bias = lax.dynamic_slice_in_dim(linear_bias, first, half * mixed_width)
            out = lax.dynamic_update_slice(
                out, (added(summed) + bias).astype(jnp.bfloat16), (starts[step], first)
            )
        return out

    return on_device


def solution(mesh):
    return jax.shard_map(
        build(mesh),
        mesh=mesh,
        in_specs=(
            P(("col", "batch"), "row"),
            P("row", ("col", "batch")),
            P("col"),
            P(),
            P("col", ("row", "batch")),
            P("row"),
        ),
        out_specs=P(("col", "batch"), "row"),
        check_vma=False,
    )
```

```python
import functools

import jax
import jax.numpy as jnp
from jax import lax
from jax.experimental import pallas as pl
from jax.experimental.pallas import tpu as pltpu
from jax.sharding import PartitionSpec as P

SHARES = (4, 4)
VMEM_BYTES = 48 * 2**20


def far_and_near(size, bit):
    return [(place, place ^ bit) for place in range(size)]


def cross_kernel(steps, first, meta, samples, *refs):
    weights, out, total = refs[:-2], refs[-2], refs[-1]
    step = lax.rem(pl.program_id(0), steps)
    piece = pl.program_id(0) // steps

    @pl.when(step == 0)
    def _():
        total[...] = jnp.zeros_like(total)

    for place, weight in enumerate(weights):

        @pl.when((piece == place) & (step < meta[(first + place) * (steps + 1)]))
        def _():
            total[...] += jnp.dot(samples[...], weight[...], preferred_element_type=jnp.float32)

    @pl.when(step == steps - 1)
    def _():
        out[...] = total[...].astype(out.dtype)


def cross_product(meta, first, samples, weights, block):
    rows, depth = samples.shape
    columns = weights[0].shape[1]
    steps = depth // block

    def listed(place, step, meta):
        return meta[(first + place) * (steps + 1) + 1 + step]

    def weight_spec(place):
        return pl.BlockSpec(
            (block, columns),
            lambda i, meta: (listed(place, jnp.clip(i - place * steps, 0, steps - 1), meta), 0),
        )

    return pl.pallas_call(
        functools.partial(cross_kernel, steps, first),
        out_shape=jax.ShapeDtypeStruct((rows, columns * len(weights)), jnp.bfloat16),
        grid_spec=pltpu.PrefetchScalarGridSpec(
            num_scalar_prefetch=1,
            grid=(len(weights) * steps,),
            in_specs=[
                pl.BlockSpec(
                    (rows, block), lambda i, meta: (0, listed(i // steps, lax.rem(i, steps), meta))
                ),
                *(weight_spec(place) for place in range(len(weights))),
            ],
            out_specs=pl.BlockSpec((rows, columns), lambda i, meta: (0, i // steps)),
            scratch_shapes=[pltpu.VMEM((rows, columns), jnp.float32)],
        ),
        compiler_params=pltpu.CompilerParams(vmem_limit_bytes=VMEM_BYTES),
        cost_estimate=pl.CostEstimate(
            flops=rows * depth * columns * len(weights),
            bytes_accessed=(rows * depth + depth * columns + 2 * rows * columns) * len(weights),
            transcendentals=0,
        ),
    )(meta, samples, *weights)


def linear_kernel(groups, parts, per_piece, meta, *refs):
    mine, theirs = refs[:groups], refs[groups : 2 * groups]
    weights, out, joined, sems = refs[2 * groups : -3], refs[-3], refs[-2], refs[-1]
    step = pl.program_id(0)
    pieces = sems.shape[0]
    width = joined.shape[1] // pieces
    in_group = pieces // groups

    @pl.when(step == 0)
    def _():
        def copy(sources, apart):
            columns = pl.ds(pl.multiple_of(meta[1 + apart] * width, width), width)
            source = sources[apart // in_group]
            first = apart % in_group * width
            return pltpu.make_async_copy(
                source.at[:, pl.ds(first, width)], joined.at[:, columns], sems.at[apart]
            )

        @pl.when(meta[0] == 1)
        def _():
            for apart in range(pieces):
                copy(mine, apart).start()
            for apart in range(pieces):
                copy(mine, apart).wait()

        @pl.when(meta[0] == 0)
        def _():
            for apart in range(pieces):
                copy(theirs, apart).start()
            for apart in range(pieces):
                copy(theirs, apart).wait()

    depth = joined.shape[1] // parts
    for place in range(len(weights) // parts):

        @pl.when(step // per_piece == place)
        def _():
            total = jnp.dot(
                joined[:, :depth], weights[place * parts][...], preferred_element_type=jnp.float32
            )
            for part in range(1, parts):
                total += jnp.dot(
                    joined[:, part * depth : (part + 1) * depth],
                    weights[place * parts + part][...],
                    preferred_element_type=jnp.float32,
                )
            out[...] = total.astype(out.dtype)


def linear_product(meta, pieces, mine, theirs, weights):
    groups, parts = len(mine), len(weights[0])
    rows = mine[0].shape[0]
    depth, columns = weights[0][0].shape
    whole_depth = depth * parts
    tile = min(columns, 512)
    per_piece = columns // tile
    anywhere = pl.BlockSpec(memory_space=pl.ANY)

    def weight_spec(place):
        return pl.BlockSpec(
            (depth, tile),
            lambda i, meta: (0, jnp.clip(i - place * per_piece, 0, per_piece - 1)),
        )

    def out_index(i, meta):
        return 0, meta[1 + pieces + i // per_piece] * per_piece + i % per_piece

    return pl.pallas_call(
        functools.partial(linear_kernel, groups, parts, per_piece),
        out_shape=jax.ShapeDtypeStruct((rows, columns * len(weights)), jnp.bfloat16),
        grid_spec=pltpu.PrefetchScalarGridSpec(
            num_scalar_prefetch=1,
            grid=(per_piece * len(weights),),
            in_specs=[anywhere] * (2 * groups)
            + [weight_spec(place) for place in range(len(weights)) for _ in range(parts)],
            out_specs=pl.BlockSpec((rows, tile), out_index),
            scratch_shapes=[
                pltpu.VMEM((rows, whole_depth), jnp.bfloat16),
                pltpu.SemaphoreType.DMA((pieces,)),
            ],
        ),
        compiler_params=pltpu.CompilerParams(vmem_limit_bytes=VMEM_BYTES),
        cost_estimate=pl.CostEstimate(
            flops=2 * rows * whole_depth * columns * len(weights),
            bytes_accessed=2 * rows * whole_depth
            + 2 * (whole_depth + rows) * columns * len(weights),
            transcendentals=0,
        ),
    )(meta, *mine, *theirs, *(part for weight in weights for part in weight))


def after(value, *others):
    return lax.optimization_barrier((value, *others))[0]


def added(*terms):
    return sum(term.astype(jnp.float32) for term in terms)


def finish_kernel(meta, own, came, samples, bias, out):
    base = samples[...].astype(jnp.float32)
    hidden = own[...].astype(jnp.float32) + came[...].astype(jnp.float32)
    out[...] = (base * (hidden + bias[...]) + base).astype(out.dtype)


def finish_cross(meta, own, came, samples, bias, pieces):
    rows, columns = own.shape[0], own.shape[1] // pieces
    part = pl.BlockSpec((rows, columns), lambda i, meta: (0, i))
    return pl.pallas_call(
        finish_kernel,
        out_shape=jax.ShapeDtypeStruct(own.shape, jnp.bfloat16),
        grid_spec=pltpu.PrefetchScalarGridSpec(
            num_scalar_prefetch=1,
            grid=(pieces,),
            in_specs=[
                part,
                part,
                pl.BlockSpec((rows, columns), lambda i, meta: (0, meta[2 * i])),
                pl.BlockSpec((1, columns), lambda i, meta: (0, meta[2 * i + 1])),
            ],
            out_specs=part,
        ),
        compiler_params=pltpu.CompilerParams(vmem_limit_bytes=VMEM_BYTES),
        cost_estimate=pl.CostEstimate(
            flops=4 * rows * columns * pieces,
            bytes_accessed=8 * rows * columns * pieces,
            transcendentals=0,
        ),
    )(meta, own, came, samples, bias)


class LineSum:
    def __init__(self, partial, place, size):
        self.partial, self.place, self.size = partial, place, size
        self.rows = partial.shape[0] // size
        self.begun = []
        if size == 4:
            inward = [(0, 1), (3, 2)]
            self.begun = [lax.ppermute(self.part(i), "col", inward) for i in (3, 2, 1)]

    def part(self, if_lower):
        upper = self.place >= self.size // 2
        first = jnp.where(upper, self.size - 1 - if_lower, if_lower) * self.rows
        return lax.dynamic_slice_in_dim(self.partial, first, self.rows, 0)

    def middle(self):
        self.over = []
        if self.size == 4:
            self.over = [
                lax.ppermute(
                    added(self.part(i), came).astype(jnp.bfloat16), "col", [(1, 2), (2, 1)]
                )
                for i, came in zip((3, 2), self.begun)
            ]
        return self.over

    def end(self):
        if self.size != 4:
            summed = lax.psum_scatter(self.partial, "col", scatter_dimension=0, tiled=True)
            return summed.astype(jnp.float32)
        over_3, over_2 = self.over
        from_1 = self.begun[2]
        out_0 = lax.ppermute(
            added(self.part(0), over_3).astype(jnp.bfloat16), "col", [(1, 0), (2, 3)]
        )
        own = lax.dynamic_slice_in_dim(self.partial, self.place * self.rows, self.rows, 0)
        is_end = (self.place == 0) | (self.place == self.size - 1)
        return added(own) + jnp.where(is_end, added(out_0), added(from_1, over_2))


def build(mesh):
    n_row, n_col, n_batch = (mesh.shape[name] for name in ("row", "col", "batch"))

    def on_device(features, cross_weight, cross_bias, pattern, linear_weight, linear_bias):
        input_width, piece_width = cross_weight.shape
        width = input_width * n_row
        output_width = piece_width * n_batch
        mixed_width = linear_weight.shape[1]
        block = width // pattern.shape[0]
        in_blocks = input_width // block
        row, col, batch = (lax.axis_index(name) for name in ("row", "col", "batch"))
        half = n_batch // 2

        def to_batch(shard, bit):
            return lax.ppermute(shard, "batch", far_and_near(n_batch, bit))

        def spread_near(pieces):
            bit = half // 2
            while bit:
                for apart in list(pieces):
                    pieces[apart | bit] = to_batch(pieces[apart], bit)
                bit //= 2
            return pieces

        cross_across = to_batch(cross_weight, half)
        parts = jnp.split(linear_weight, 2, axis=0)
        linear_across = [to_batch(part, half) for part in parts]
        cross_pieces = spread_near({0: cross_weight})
        linear_pieces = {
            place: [piece] for place, piece in spread_near({0: linear_weight}).items()
        }

        shard_rows = features.shape[0]
        starts = [shard_rows * sum(SHARES[:i]) // sum(SHARES) for i in range(len(SHARES) + 1)]
        shards = [features[first:last] for first, last in zip(starts, starts[1:])]
        gathered = [lax.all_gather(shard, "col", axis=0, tiled=True) for shard in shards]

        def kept_list(apart):
            out_block = (col * n_batch + (batch ^ apart)) * piece_width // block
            kept = lax.dynamic_slice(pattern, (out_block, row * in_blocks), (1, in_blocks))[0]
            number = jnp.sum(kept)
            rank = jnp.cumsum(kept) - 1
            slots = jnp.minimum(jnp.arange(in_blocks), jnp.maximum(number - 1, 0))
            match = (rank[None, :] == slots[:, None]) & (kept[None, :] == 1)
            listed = jnp.sum(jnp.where(match, jnp.arange(in_blocks)[None, :], 0), axis=1)
            return jnp.concatenate([number[None], listed]).astype(jnp.int32)

        kept_lists = [kept_list(apart) for apart in range(n_batch)]

        def owner_of(column):
            return column * output_width // input_width

        is_owner = row == col * output_width // input_width
        turns = [
            [
                ((owner_of(c) + turn) % n_row * n_col + c, owner_of(c) * n_col + c)
                for c in range(n_col)
            ]
            for turn in range(1, n_row)
        ]
        first_base = jnp.where(is_owner, col * output_width - row * input_width, 0)

        chunks = range(len(SHARES))
        bias_row = cross_bias[None, :]
        near, far = 0, 1
        in_group = [list(range(half)), list(range(half, n_batch))]
        places = {}
        for group in (near, far):
            listed = []
            for apart in in_group[group]:
                listed += [first_base // piece_width + (batch ^ apart), batch ^ apart]
            places[group] = jnp.stack(listed)
        products, came, mine, theirs, partial = {}, {}, {}, {}, {}
        latest = []
        lists = jnp.concatenate(kept_lists).astype(jnp.int32)
        lists = after(lists, *parts)

        def in_turn(meta, *others):
            return after(meta.astype(jnp.int32), *latest[-1:], *others)

        def multiply(step, group, *others, send=True):
            product = cross_product(
                in_turn(lists, *others),
                in_group[group][0],
                gathered[step],
                [cross_pieces[apart] for apart in in_group[group]],
                block,
            )
            latest.append(product)
            products[step, group] = product
            if send:
                sent = [lax.ppermute(product, ("row", "col"), pairs) for pairs in turns]
                came[step, group] = sum(sent[1:], sent[0])

        def finish(step, group, *others, beside=None):
            crossed = finish_cross(
                in_turn(places[group], *others),
                products[step, group],
                came[step, group],
                gathered[step],
                bias_row,
                half,
            )
            latest.append(crossed)
            returns = [[(to, source) for source, to in pairs] for pairs in turns]
            sent = crossed
            if beside is not None:
                sent = jnp.where(is_owner, crossed, products[step, beside])
                returns = [back + pairs for back, pairs in zip(returns, turns)]
            back = [lax.ppermute(sent, ("row", "col"), pairs) for pairs in returns]
            mine[step, group], theirs[step, group] = crossed, sum(back[1:], back[0])
            if beside is not None:
                came[step, beside] = theirs[step, group]

        meta = jnp.stack(
            [is_owner.astype(jnp.int32)]
            + [batch ^ place for place in range(n_batch)]
            + [(batch ^ place) % half for place in range(half)]
        )

        def linear(step, group, *others):
            product = linear_product(
                in_turn(meta, *others),
                n_batch,
                [mine[step, g] for g in (near, far)],
                [theirs[step, g] for g in (near, far)],
                [linear_pieces[apart] for apart in in_group[group]],
            )
            latest.append(product)
            partial[step, group] = product

        def spread_far_cross(*others):
            arrived = spread_near({0: after(cross_across, *others)})
            cross_pieces.update({half + place: arrived[place] for place in range(half)})

        def spread_far_linear(across):
            arrived = [spread_near({0: part}) for part in across]
            for place in range(half):
                linear_pieces[half + place] = [part[place] for part in arrived]

        begun = {}
        multiply(0, near)
        spread_far_cross(latest[-1])
        multiply(0, far)
        finish(0, near, *(linear_pieces[place][0] for place in range(half)))
        finish(0, far)
        multiply(1, near, linear_across[0])
        multiply(1, far, send=False)
        linear(0, near)
        summed_first = lax.psum_scatter(
            partial[0, near], "col", scatter_dimension=0, tiled=True
        )
        finish(1, near, beside=far)
        finish(1, far)
        linear_across = [after(part, latest[-1]) for part in linear_across]
        spread_far_linear(linear_across)
        linear(0, far, summed_first, theirs[1, far])
        begun[0] = LineSum(partial[0, far], col, n_col)
        linear(1, near)
        linear(1, far, *begun[0].begun[:1])
        begun[1] = LineSum(partial[1, far], col, n_col)
        begun[0].middle()
        begun[1].middle()

        out = jnp.zeros((shard_rows, mixed_width * n_batch), jnp.bfloat16)
        for step, group in ((0, near), (0, far), (1, far), (1, near)):
            if group == far:
                summed = begun[step].end()
            elif step == 0:
                summed = summed_first
            else:
                summed = lax.psum_scatter(
                    partial[step, group], "col", scatter_dimension=0, tiled=True
                )
            first = ((batch // half) ^ group) * half * mixed_width
            bias = lax.dynamic_slice_in_dim(linear_bias, first, half * mixed_width)
            out = lax.dynamic_update_slice(
                out, (added(summed) + bias).astype(jnp.bfloat16), (starts[step], first)
            )
        return out

    return on_device


def solution(mesh):
    return jax.shard_map(
        build(mesh),
        mesh=mesh,
        in_specs=(
            P(("col", "batch"), "row"),
            P("row", ("col", "batch")),
            P("col"),
            P(),
            P("col", ("row", "batch")),
            P("row"),
        ),
        out_specs=P(("col", "batch"), "row"),
        check_vma=False,
    )
```

```python
import functools

import jax
import jax.numpy as jnp
from jax import lax
from jax.experimental import pallas as pl
from jax.experimental.pallas import tpu as pltpu
from jax.sharding import PartitionSpec as P

SHARES = (4, 4)
VMEM_BYTES = 48 * 2**20


def far_and_near(size, bit):
    return [(place, place ^ bit) for place in range(size)]


def cross_kernel(steps, first, meta, samples, *refs):
    weights, out, total = refs[:-2], refs[-2], refs[-1]
    step = lax.rem(pl.program_id(0), steps)
    piece = pl.program_id(0) // steps

    @pl.when(step == 0)
    def _():
        total[...] = jnp.zeros_like(total)

    for place, weight in enumerate(weights):

        @pl.when((piece == place) & (step < meta[(first + place) * (steps + 1)]))
        def _():
            total[...] += jnp.dot(samples[...], weight[...], preferred_element_type=jnp.float32)

    @pl.when(step == steps - 1)
    def _():
        out[...] = total[...].astype(out.dtype)


def cross_product(meta, first, samples, weights, block):
    rows, depth = samples.shape
    columns = weights[0].shape[1]
    steps = depth // block

    def listed(place, step, meta):
        return meta[(first + place) * (steps + 1) + 1 + step]

    def weight_spec(place):
        return pl.BlockSpec(
            (block, columns),
            lambda i, meta: (listed(place, jnp.clip(i - place * steps, 0, steps - 1), meta), 0),
        )

    return pl.pallas_call(
        functools.partial(cross_kernel, steps, first),
        out_shape=jax.ShapeDtypeStruct((rows, columns * len(weights)), jnp.bfloat16),
        grid_spec=pltpu.PrefetchScalarGridSpec(
            num_scalar_prefetch=1,
            grid=(len(weights) * steps,),
            in_specs=[
                pl.BlockSpec(
                    (rows, block), lambda i, meta: (0, listed(i // steps, lax.rem(i, steps), meta))
                ),
                *(weight_spec(place) for place in range(len(weights))),
            ],
            out_specs=pl.BlockSpec((rows, columns), lambda i, meta: (0, i // steps)),
            scratch_shapes=[pltpu.VMEM((rows, columns), jnp.float32)],
        ),
        compiler_params=pltpu.CompilerParams(vmem_limit_bytes=VMEM_BYTES),
        cost_estimate=pl.CostEstimate(
            flops=rows * depth * columns * len(weights),
            bytes_accessed=(rows * depth + depth * columns + 2 * rows * columns) * len(weights),
            transcendentals=0,
        ),
    )(meta, samples, *weights)


def linear_kernel(groups, parts, per_piece, meta, *refs):
    mine, theirs = refs[:groups], refs[groups : 2 * groups]
    weights, out, joined, sems = refs[2 * groups : -3], refs[-3], refs[-2], refs[-1]
    step = pl.program_id(0)
    pieces = sems.shape[0]
    width = joined.shape[1] // pieces
    in_group = pieces // groups

    @pl.when(step == 0)
    def _():
        def copy(sources, apart):
            columns = pl.ds(pl.multiple_of(meta[1 + apart] * width, width), width)
            source = sources[apart // in_group]
            first = apart % in_group * width
            return pltpu.make_async_copy(
                source.at[:, pl.ds(first, width)], joined.at[:, columns], sems.at[apart]
            )

        @pl.when(meta[0] == 1)
        def _():
            for apart in range(pieces):
                copy(mine, apart).start()
            for apart in range(pieces):
                copy(mine, apart).wait()

        @pl.when(meta[0] == 0)
        def _():
            for apart in range(pieces):
                copy(theirs, apart).start()
            for apart in range(pieces):
                copy(theirs, apart).wait()

    depth = joined.shape[1] // parts
    for place in range(len(weights) // parts):

        @pl.when(step // per_piece == place)
        def _():
            total = jnp.dot(
                joined[:, :depth], weights[place * parts][...], preferred_element_type=jnp.float32
            )
            for part in range(1, parts):
                total += jnp.dot(
                    joined[:, part * depth : (part + 1) * depth],
                    weights[place * parts + part][...],
                    preferred_element_type=jnp.float32,
                )
            out[...] = total.astype(out.dtype)


def linear_product(meta, pieces, mine, theirs, weights):
    groups, parts = len(mine), len(weights[0])
    rows = mine[0].shape[0]
    depth, columns = weights[0][0].shape
    whole_depth = depth * parts
    tile = min(columns, 512)
    per_piece = columns // tile
    anywhere = pl.BlockSpec(memory_space=pl.ANY)

    def weight_spec(place):
        return pl.BlockSpec(
            (depth, tile),
            lambda i, meta: (0, jnp.clip(i - place * per_piece, 0, per_piece - 1)),
        )

    def out_index(i, meta):
        return 0, meta[1 + pieces + i // per_piece] * per_piece + i % per_piece

    return pl.pallas_call(
        functools.partial(linear_kernel, groups, parts, per_piece),
        out_shape=jax.ShapeDtypeStruct((rows, columns * len(weights)), jnp.bfloat16),
        grid_spec=pltpu.PrefetchScalarGridSpec(
            num_scalar_prefetch=1,
            grid=(per_piece * len(weights),),
            in_specs=[anywhere] * (2 * groups)
            + [weight_spec(place) for place in range(len(weights)) for _ in range(parts)],
            out_specs=pl.BlockSpec((rows, tile), out_index),
            scratch_shapes=[
                pltpu.VMEM((rows, whole_depth), jnp.bfloat16),
                pltpu.SemaphoreType.DMA((pieces,)),
            ],
        ),
        compiler_params=pltpu.CompilerParams(vmem_limit_bytes=VMEM_BYTES),
        cost_estimate=pl.CostEstimate(
            flops=2 * rows * whole_depth * columns * len(weights),
            bytes_accessed=2 * rows * whole_depth
            + 2 * (whole_depth + rows) * columns * len(weights),
            transcendentals=0,
        ),
    )(meta, *mine, *theirs, *(part for weight in weights for part in weight))


def after(value, *others):
    return lax.optimization_barrier((value, *others))[0]


def added(*terms):
    return sum(term.astype(jnp.float32) for term in terms)


def finish_kernel(meta, own, came, samples, bias, out):
    base = samples[...].astype(jnp.float32)
    hidden = own[...].astype(jnp.float32) + came[...].astype(jnp.float32)
    out[...] = (base * (hidden + bias[...]) + base).astype(out.dtype)


def finish_cross(meta, own, came, samples, bias, pieces):
    rows, columns = own.shape[0], own.shape[1] // pieces
    part = pl.BlockSpec((rows, columns), lambda i, meta: (0, i))
    return pl.pallas_call(
        finish_kernel,
        out_shape=jax.ShapeDtypeStruct(own.shape, jnp.bfloat16),
        grid_spec=pltpu.PrefetchScalarGridSpec(
            num_scalar_prefetch=1,
            grid=(pieces,),
            in_specs=[
                part,
                part,
                pl.BlockSpec((rows, columns), lambda i, meta: (0, meta[2 * i])),
                pl.BlockSpec((1, columns), lambda i, meta: (0, meta[2 * i + 1])),
            ],
            out_specs=part,
        ),
        compiler_params=pltpu.CompilerParams(vmem_limit_bytes=VMEM_BYTES),
        cost_estimate=pl.CostEstimate(
            flops=4 * rows * columns * pieces,
            bytes_accessed=8 * rows * columns * pieces,
            transcendentals=0,
        ),
    )(meta, own, came, samples, bias)


class LineSum:
    def __init__(self, partial, place, size):
        self.partial, self.place, self.size = partial, place, size
        self.rows = partial.shape[0] // size
        self.begun = []
        if size == 4:
            inward = [(0, 1), (3, 2)]
            self.begun = [lax.ppermute(self.part(i), "col", inward) for i in (3, 2, 1)]

    def part(self, if_lower):
        upper = self.place >= self.size // 2
        first = jnp.where(upper, self.size - 1 - if_lower, if_lower) * self.rows
        return lax.dynamic_slice_in_dim(self.partial, first, self.rows, 0)

    def middle(self):
        self.over = []
        if self.size == 4:
            self.over = [
                lax.ppermute(
                    added(self.part(i), came).astype(jnp.bfloat16), "col", [(1, 2), (2, 1)]
                )
                for i, came in zip((3, 2), self.begun)
            ]
        return self.over

    def end(self):
        if self.size != 4:
            summed = lax.psum_scatter(self.partial, "col", scatter_dimension=0, tiled=True)
            return summed.astype(jnp.float32)
        over_3, over_2 = self.over
        from_1 = self.begun[2]
        out_0 = lax.ppermute(
            added(self.part(0), over_3).astype(jnp.bfloat16), "col", [(1, 0), (2, 3)]
        )
        own = lax.dynamic_slice_in_dim(self.partial, self.place * self.rows, self.rows, 0)
        is_end = (self.place == 0) | (self.place == self.size - 1)
        return added(own) + jnp.where(is_end, added(out_0), added(from_1, over_2))


def build(mesh):
    n_row, n_col, n_batch = (mesh.shape[name] for name in ("row", "col", "batch"))

    def on_device(features, cross_weight, cross_bias, pattern, linear_weight, linear_bias):
        input_width, piece_width = cross_weight.shape
        width = input_width * n_row
        output_width = piece_width * n_batch
        mixed_width = linear_weight.shape[1]
        block = width // pattern.shape[0]
        in_blocks = input_width // block
        row, col, batch = (lax.axis_index(name) for name in ("row", "col", "batch"))
        half = n_batch // 2

        def to_batch(shard, bit):
            return lax.ppermute(shard, "batch", far_and_near(n_batch, bit))

        def spread_near(pieces):
            bit = half // 2
            while bit:
                for apart in list(pieces):
                    pieces[apart | bit] = to_batch(pieces[apart], bit)
                bit //= 2
            return pieces

        cross_across = to_batch(cross_weight, half)
        parts = jnp.split(linear_weight, 2, axis=0)
        linear_across = [to_batch(part, half) for part in parts]
        cross_pieces = spread_near({0: cross_weight})
        linear_pieces = {
            place: [piece] for place, piece in spread_near({0: linear_weight}).items()
        }

        shard_rows = features.shape[0]
        starts = [shard_rows * sum(SHARES[:i]) // sum(SHARES) for i in range(len(SHARES) + 1)]
        shards = [features[first:last] for first, last in zip(starts, starts[1:])]
        gathered = [lax.all_gather(shard, "col", axis=0, tiled=True) for shard in shards]

        def kept_list(apart):
            out_block = (col * n_batch + (batch ^ apart)) * piece_width // block
            kept = lax.dynamic_slice(pattern, (out_block, row * in_blocks), (1, in_blocks))[0]
            number = jnp.sum(kept)
            rank = jnp.cumsum(kept) - 1
            slots = jnp.minimum(jnp.arange(in_blocks), jnp.maximum(number - 1, 0))
            match = (rank[None, :] == slots[:, None]) & (kept[None, :] == 1)
            listed = jnp.sum(jnp.where(match, jnp.arange(in_blocks)[None, :], 0), axis=1)
            return jnp.concatenate([number[None], listed]).astype(jnp.int32)

        kept_lists = [kept_list(apart) for apart in range(n_batch)]

        def owner_of(column):
            return column * output_width // input_width

        is_owner = row == col * output_width // input_width
        turns = [
            [
                ((owner_of(c) + turn) % n_row * n_col + c, owner_of(c) * n_col + c)
                for c in range(n_col)
            ]
            for turn in range(1, n_row)
        ]
        first_base = jnp.where(is_owner, col * output_width - row * input_width, 0)

        chunks = range(len(SHARES))
        bias_row = cross_bias[None, :]
        near, far = 0, 1
        in_group = [list(range(half)), list(range(half, n_batch))]
        places = {}
        for group in (near, far):
            listed = []
            for apart in in_group[group]:
                listed += [first_base // piece_width + (batch ^ apart), batch ^ apart]
            places[group] = jnp.stack(listed)
        products, came, mine, theirs, partial = {}, {}, {}, {}, {}
        latest = []
        lists = jnp.concatenate(kept_lists).astype(jnp.int32)
        lists = after(lists, *parts)

        def in_turn(meta, *others):
            return after(meta.astype(jnp.int32), *latest[-1:], *others)

        def multiply(step, group, *others, send=True):
            product = cross_product(
                in_turn(lists, *others),
                in_group[group][0],
                gathered[step],
                [cross_pieces[apart] for apart in in_group[group]],
                block,
            )
            latest.append(product)
            products[step, group] = product
            if send:
                sent = [lax.ppermute(product, ("row", "col"), pairs) for pairs in turns]
                came[step, group] = sum(sent[1:], sent[0])

        def finish(step, group, *others, beside=None):
            crossed = finish_cross(
                in_turn(places[group], *others),
                products[step, group],
                came[step, group],
                gathered[step],
                bias_row,
                half,
            )
            latest.append(crossed)
            returns = [[(to, source) for source, to in pairs] for pairs in turns]
            sent = crossed
            if beside is not None:
                sent = jnp.where(is_owner, crossed, products[step, beside])
                returns = [back + pairs for back, pairs in zip(returns, turns)]
            back = [lax.ppermute(sent, ("row", "col"), pairs) for pairs in returns]
            mine[step, group], theirs[step, group] = crossed, sum(back[1:], back[0])
            if beside is not None:
                came[step, beside] = theirs[step, group]

        meta = jnp.stack(
            [is_owner.astype(jnp.int32)]
            + [batch ^ place for place in range(n_batch)]
            + [(batch ^ place) % half for place in range(half)]
        )

        def linear(step, group, *others):
            product = linear_product(
                in_turn(meta, *others),
                n_batch,
                [mine[step, g] for g in (near, far)],
                [theirs[step, g] for g in (near, far)],
                [linear_pieces[apart] for apart in in_group[group]],
            )
            latest.append(product)
            partial[step, group] = product

        def spread_far_cross(*others):
            arrived = spread_near({0: after(cross_across, *others)})
            cross_pieces.update({half + place: arrived[place] for place in range(half)})

        def spread_far_linear(across):
            arrived = [spread_near({0: part}) for part in across]
            for place in range(half):
                linear_pieces[half + place] = [part[place] for part in arrived]

        begun = {}
        multiply(0, near)
        spread_far_cross(latest[-1])
        multiply(0, far)
        finish(0, near, *(linear_pieces[place][0] for place in range(half)))
        finish(0, far)
        multiply(1, near, linear_across[0])
        multiply(1, far, send=False)
        linear(0, near)
        summed_first = lax.psum_scatter(
            partial[0, near], "col", scatter_dimension=0, tiled=True
        )
        finish(1, near, beside=far)
        finish(1, far)
        linear_across = [after(part, latest[-1]) for part in linear_across]
        spread_far_linear(linear_across)
        linear(0, far, summed_first)
        summed_far = lax.psum_scatter(partial[0, far], "col", scatter_dimension=0, tiled=True)
        linear(1, near)
        linear(1, far)
        begun[1] = LineSum(partial[1, far], col, n_col)
        begun[1].begun[:1] = [after(value, summed_far) for value in begun[1].begun[:1]]
        begun[1].middle()

        out = jnp.zeros((shard_rows, mixed_width * n_batch), jnp.bfloat16)
        for step, group in ((0, near), (0, far), (1, far), (1, near)):
            if step == 0:
                summed = summed_far if group == far else summed_first
            elif group == far:
                summed = begun[step].end()
            else:
                summed = lax.psum_scatter(
                    partial[step, group], "col", scatter_dimension=0, tiled=True
                )
            first = ((batch // half) ^ group) * half * mixed_width
            bias = lax.dynamic_slice_in_dim(linear_bias, first, half * mixed_width)
            out = lax.dynamic_update_slice(
                out, (added(summed) + bias).astype(jnp.bfloat16), (starts[step], first)
            )
        return out

    return on_device


def solution(mesh):
    return jax.shard_map(
        build(mesh),
        mesh=mesh,
        in_specs=(
            P(("col", "batch"), "row"),
            P("row", ("col", "batch")),
            P("col"),
            P(),
            P("col", ("row", "batch")),
            P("row"),
        ),
        out_specs=P(("col", "batch"), "row"),
        check_vma=False,
    )
```

```python
import functools

import jax
import jax.numpy as jnp
from jax import lax
from jax.experimental import pallas as pl
from jax.experimental.pallas import tpu as pltpu
from jax.sharding import PartitionSpec as P

SHARES = (4, 4)
VMEM_BYTES = 48 * 2**20


def far_and_near(size, bit):
    return [(place, place ^ bit) for place in range(size)]


def cross_kernel(steps, first, meta, samples, *refs):
    weights, out, total = refs[:-2], refs[-2], refs[-1]
    step = lax.rem(pl.program_id(0), steps)
    piece = pl.program_id(0) // steps

    @pl.when(step == 0)
    def _():
        total[...] = jnp.zeros_like(total)

    for place, weight in enumerate(weights):

        @pl.when((piece == place) & (step < meta[(first + place) * (steps + 1)]))
        def _():
            total[...] += jnp.dot(samples[...], weight[...], preferred_element_type=jnp.float32)

    @pl.when(step == steps - 1)
    def _():
        out[...] = total[...].astype(out.dtype)


def cross_product(meta, first, samples, weights, block):
    rows, depth = samples.shape
    columns = weights[0].shape[1]
    steps = depth // block

    def listed(place, step, meta):
        return meta[(first + place) * (steps + 1) + 1 + step]

    def weight_spec(place):
        return pl.BlockSpec(
            (block, columns),
            lambda i, meta: (listed(place, jnp.clip(i - place * steps, 0, steps - 1), meta), 0),
        )

    return pl.pallas_call(
        functools.partial(cross_kernel, steps, first),
        out_shape=jax.ShapeDtypeStruct((rows, columns * len(weights)), jnp.bfloat16),
        grid_spec=pltpu.PrefetchScalarGridSpec(
            num_scalar_prefetch=1,
            grid=(len(weights) * steps,),
            in_specs=[
                pl.BlockSpec(
                    (rows, block), lambda i, meta: (0, listed(i // steps, lax.rem(i, steps), meta))
                ),
                *(weight_spec(place) for place in range(len(weights))),
            ],
            out_specs=pl.BlockSpec((rows, columns), lambda i, meta: (0, i // steps)),
            scratch_shapes=[pltpu.VMEM((rows, columns), jnp.float32)],
        ),
        compiler_params=pltpu.CompilerParams(vmem_limit_bytes=VMEM_BYTES),
        cost_estimate=pl.CostEstimate(
            flops=rows * depth * columns * len(weights),
            bytes_accessed=(rows * depth + depth * columns + 2 * rows * columns) * len(weights),
            transcendentals=0,
        ),
    )(meta, samples, *weights)


def linear_kernel(groups, parts, per_piece, meta, *refs):
    mine, theirs = refs[:groups], refs[groups : 2 * groups]
    weights, out, joined, sems = refs[2 * groups : -3], refs[-3], refs[-2], refs[-1]
    step = pl.program_id(0)
    pieces = sems.shape[0]
    width = joined.shape[1] // pieces
    in_group = pieces // groups

    @pl.when(step == 0)
    def _():
        def copy(sources, apart):
            columns = pl.ds(pl.multiple_of(meta[1 + apart] * width, width), width)
            source = sources[apart // in_group]
            first = apart % in_group * width
            return pltpu.make_async_copy(
                source.at[:, pl.ds(first, width)], joined.at[:, columns], sems.at[apart]
            )

        @pl.when(meta[0] == 1)
        def _():
            for apart in range(pieces):
                copy(mine, apart).start()
            for apart in range(pieces):
                copy(mine, apart).wait()

        @pl.when(meta[0] == 0)
        def _():
            for apart in range(pieces):
                copy(theirs, apart).start()
            for apart in range(pieces):
                copy(theirs, apart).wait()

    depth = joined.shape[1] // parts
    for place in range(len(weights) // parts):

        @pl.when(step // per_piece == place)
        def _():
            total = jnp.dot(
                joined[:, :depth], weights[place * parts][...], preferred_element_type=jnp.float32
            )
            for part in range(1, parts):
                total += jnp.dot(
                    joined[:, part * depth : (part + 1) * depth],
                    weights[place * parts + part][...],
                    preferred_element_type=jnp.float32,
                )
            out[...] = total.astype(out.dtype)


def linear_product(meta, pieces, mine, theirs, weights):
    groups, parts = len(mine), len(weights[0])
    rows = mine[0].shape[0]
    depth, columns = weights[0][0].shape
    whole_depth = depth * parts
    tile = min(columns, 512)
    per_piece = columns // tile
    anywhere = pl.BlockSpec(memory_space=pl.ANY)

    def weight_spec(place):
        return pl.BlockSpec(
            (depth, tile),
            lambda i, meta: (0, jnp.clip(i - place * per_piece, 0, per_piece - 1)),
        )

    def out_index(i, meta):
        return 0, meta[1 + pieces + i // per_piece] * per_piece + i % per_piece

    return pl.pallas_call(
        functools.partial(linear_kernel, groups, parts, per_piece),
        out_shape=jax.ShapeDtypeStruct((rows, columns * len(weights)), jnp.bfloat16),
        grid_spec=pltpu.PrefetchScalarGridSpec(
            num_scalar_prefetch=1,
            grid=(per_piece * len(weights),),
            in_specs=[anywhere] * (2 * groups)
            + [weight_spec(place) for place in range(len(weights)) for _ in range(parts)],
            out_specs=pl.BlockSpec((rows, tile), out_index),
            scratch_shapes=[
                pltpu.VMEM((rows, whole_depth), jnp.bfloat16),
                pltpu.SemaphoreType.DMA((pieces,)),
            ],
        ),
        compiler_params=pltpu.CompilerParams(vmem_limit_bytes=VMEM_BYTES),
        cost_estimate=pl.CostEstimate(
            flops=2 * rows * whole_depth * columns * len(weights),
            bytes_accessed=2 * rows * whole_depth
            + 2 * (whole_depth + rows) * columns * len(weights),
            transcendentals=0,
        ),
    )(meta, *mine, *theirs, *(part for weight in weights for part in weight))


def after(value, *others):
    return lax.optimization_barrier((value, *others))[0]


def added(*terms):
    return sum(term.astype(jnp.float32) for term in terms)


def finish_kernel(meta, own, came, samples, bias, out):
    base = samples[...].astype(jnp.float32)
    hidden = own[...].astype(jnp.float32) + came[...].astype(jnp.float32)
    out[...] = (base * (hidden + bias[...]) + base).astype(out.dtype)


def finish_cross(meta, own, came, samples, bias, pieces):
    rows, columns = own.shape[0], own.shape[1] // pieces
    part = pl.BlockSpec((rows, columns), lambda i, meta: (0, i))
    return pl.pallas_call(
        finish_kernel,
        out_shape=jax.ShapeDtypeStruct(own.shape, jnp.bfloat16),
        grid_spec=pltpu.PrefetchScalarGridSpec(
            num_scalar_prefetch=1,
            grid=(pieces,),
            in_specs=[
                part,
                part,
                pl.BlockSpec((rows, columns), lambda i, meta: (0, meta[2 * i])),
                pl.BlockSpec((1, columns), lambda i, meta: (0, meta[2 * i + 1])),
            ],
            out_specs=part,
        ),
        compiler_params=pltpu.CompilerParams(vmem_limit_bytes=VMEM_BYTES),
        cost_estimate=pl.CostEstimate(
            flops=4 * rows * columns * pieces,
            bytes_accessed=8 * rows * columns * pieces,
            transcendentals=0,
        ),
    )(meta, own, came, samples, bias)


class LineSum:
    def __init__(self, partial, place, size):
        self.partial, self.place, self.size = partial, place, size
        self.rows = partial.shape[0] // size
        self.begun = []
        if size == 4:
            inward = [(0, 1), (3, 2)]
            self.begun = [lax.ppermute(self.part(i), "col", inward) for i in (3, 2, 1)]

    def part(self, if_lower):
        upper = self.place >= self.size // 2
        first = jnp.where(upper, self.size - 1 - if_lower, if_lower) * self.rows
        return lax.dynamic_slice_in_dim(self.partial, first, self.rows, 0)

    def middle(self):
        self.over = []
        if self.size == 4:
            self.over = [
                lax.ppermute(
                    added(self.part(i), came).astype(jnp.bfloat16), "col", [(1, 2), (2, 1)]
                )
                for i, came in zip((3, 2), self.begun)
            ]
        return self.over

    def end(self):
        if self.size != 4:
            summed = lax.psum_scatter(self.partial, "col", scatter_dimension=0, tiled=True)
            return summed.astype(jnp.float32)
        over_3, over_2 = self.over
        from_1 = self.begun[2]
        out_0 = lax.ppermute(
            added(self.part(0), over_3).astype(jnp.bfloat16), "col", [(1, 0), (2, 3)]
        )
        own = lax.dynamic_slice_in_dim(self.partial, self.place * self.rows, self.rows, 0)
        is_end = (self.place == 0) | (self.place == self.size - 1)
        return added(own) + jnp.where(is_end, added(out_0), added(from_1, over_2))


def build(mesh):
    n_row, n_col, n_batch = (mesh.shape[name] for name in ("row", "col", "batch"))

    def on_device(features, cross_weight, cross_bias, pattern, linear_weight, linear_bias):
        input_width, piece_width = cross_weight.shape
        width = input_width * n_row
        output_width = piece_width * n_batch
        mixed_width = linear_weight.shape[1]
        block = width // pattern.shape[0]
        in_blocks = input_width // block
        row, col, batch = (lax.axis_index(name) for name in ("row", "col", "batch"))
        half = n_batch // 2

        def to_batch(shard, bit):
            return lax.ppermute(shard, "batch", far_and_near(n_batch, bit))

        def spread_near(pieces):
            bit = half // 2
            while bit:
                for apart in list(pieces):
                    pieces[apart | bit] = to_batch(pieces[apart], bit)
                bit //= 2
            return pieces

        cross_across = to_batch(cross_weight, half)
        parts = jnp.split(linear_weight, 2, axis=0)
        linear_across = [to_batch(part, half) for part in parts]
        cross_pieces = spread_near({0: cross_weight})
        linear_pieces = {
            place: [piece] for place, piece in spread_near({0: linear_weight}).items()
        }

        shard_rows = features.shape[0]
        starts = [shard_rows * sum(SHARES[:i]) // sum(SHARES) for i in range(len(SHARES) + 1)]
        shards = [features[first:last] for first, last in zip(starts, starts[1:])]
        gathered = [lax.all_gather(shard, "col", axis=0, tiled=True) for shard in shards]

        def kept_list(apart):
            out_block = (col * n_batch + (batch ^ apart)) * piece_width // block
            kept = lax.dynamic_slice(pattern, (out_block, row * in_blocks), (1, in_blocks))[0]
            number = jnp.sum(kept)
            rank = jnp.cumsum(kept) - 1
            slots = jnp.minimum(jnp.arange(in_blocks), jnp.maximum(number - 1, 0))
            match = (rank[None, :] == slots[:, None]) & (kept[None, :] == 1)
            listed = jnp.sum(jnp.where(match, jnp.arange(in_blocks)[None, :], 0), axis=1)
            return jnp.concatenate([number[None], listed]).astype(jnp.int32)

        kept_lists = [kept_list(apart) for apart in range(n_batch)]

        def owner_of(column):
            return column * output_width // input_width

        is_owner = row == col * output_width // input_width
        turns = [
            [
                ((owner_of(c) + turn) % n_row * n_col + c, owner_of(c) * n_col + c)
                for c in range(n_col)
            ]
            for turn in range(1, n_row)
        ]
        first_base = jnp.where(is_owner, col * output_width - row * input_width, 0)

        chunks = range(len(SHARES))
        bias_row = cross_bias[None, :]
        near, far = 0, 1
        in_group = [list(range(half)), list(range(half, n_batch))]
        places = {}
        for group in (near, far):
            listed = []
            for apart in in_group[group]:
                listed += [first_base // piece_width + (batch ^ apart), batch ^ apart]
            places[group] = jnp.stack(listed)
        products, came, mine, theirs, partial = {}, {}, {}, {}, {}
        latest = []
        lists = jnp.concatenate(kept_lists).astype(jnp.int32)
        lists = after(lists, *parts)

        def in_turn(meta, *others):
            return after(meta.astype(jnp.int32), *latest[-1:], *others)

        def multiply(step, group, *others, send=True):
            product = cross_product(
                in_turn(lists, *others),
                in_group[group][0],
                gathered[step],
                [cross_pieces[apart] for apart in in_group[group]],
                block,
            )
            latest.append(product)
            products[step, group] = product
            if send:
                sent = [lax.ppermute(product, ("row", "col"), pairs) for pairs in turns]
                came[step, group] = sum(sent[1:], sent[0])

        def finish(step, group, *others, beside=None):
            crossed = finish_cross(
                in_turn(places[group], *others),
                products[step, group],
                came[step, group],
                gathered[step],
                bias_row,
                half,
            )
            latest.append(crossed)
            returns = [[(to, source) for source, to in pairs] for pairs in turns]
            sent = crossed
            if beside is not None:
                sent = jnp.where(is_owner, crossed, products[step, beside])
                returns = [back + pairs for back, pairs in zip(returns, turns)]
            back = [lax.ppermute(sent, ("row", "col"), pairs) for pairs in returns]
            mine[step, group], theirs[step, group] = crossed, sum(back[1:], back[0])
            if beside is not None:
                came[step, beside] = theirs[step, group]

        meta = jnp.stack(
            [is_owner.astype(jnp.int32)]
            + [batch ^ place for place in range(n_batch)]
            + [(batch ^ place) % half for place in range(half)]
        )

        def linear(step, group, *others):
            product = linear_product(
                in_turn(meta, *others),
                n_batch,
                [mine[step, g] for g in (near, far)],
                [theirs[step, g] for g in (near, far)],
                [linear_pieces[apart] for apart in in_group[group]],
            )
            latest.append(product)
            partial[step, group] = product

        def spread_far_cross(*others):
            arrived = spread_near({0: after(cross_across, *others)})
            cross_pieces.update({half + place: arrived[place] for place in range(half)})

        def spread_far_linear(across):
            arrived = [spread_near({0: part}) for part in across]
            for place in range(half):
                linear_pieces[half + place] = [part[place] for part in arrived]

        begun = {}
        multiply(0, near)
        spread_far_cross(latest[-1])
        multiply(0, far)
        finish(0, near, *(linear_pieces[place][0] for place in range(half)))
        finish(0, far)
        multiply(1, near, linear_across[0])
        multiply(1, far, send=False)
        linear(0, near)
        summed_first = lax.psum_scatter(
            partial[0, near], "col", scatter_dimension=0, tiled=True
        )
        finish(1, near, beside=far)
        finish(1, far)
        linear_across = [after(part, latest[-1]) for part in linear_across]
        spread_far_linear(linear_across)
        linear(0, far, summed_first)
        summed_far = lax.psum_scatter(partial[0, far], "col", scatter_dimension=0, tiled=True)
        linear(1, far)
        begun[1] = LineSum(partial[1, far], col, n_col)
        linear(1, near)
        begun[1].begun[:1] = [after(value, summed_far, partial[1, near]) for value in begun[1].begun[:1]]
        begun[1].middle()

        out = jnp.zeros((shard_rows, mixed_width * n_batch), jnp.bfloat16)
        for step, group in ((0, near), (0, far), (1, far), (1, near)):
            if step == 0:
                summed = summed_far if group == far else summed_first
            elif group == far:
                summed = begun[step].end()
            else:
                summed = lax.psum_scatter(
                    partial[step, group], "col", scatter_dimension=0, tiled=True
                )
            first = ((batch // half) ^ group) * half * mixed_width
            bias = lax.dynamic_slice_in_dim(linear_bias, first, half * mixed_width)
            out = lax.dynamic_update_slice(
                out, (added(summed) + bias).astype(jnp.bfloat16), (starts[step], first)
            )
        return out

    return on_device


def solution(mesh):
    return jax.shard_map(
        build(mesh),
        mesh=mesh,
        in_specs=(
            P(("col", "batch"), "row"),
            P("row", ("col", "batch")),
            P("col"),
            P(),
            P("col", ("row", "batch")),
            P("row"),
        ),
        out_specs=P(("col", "batch"), "row"),
        check_vma=False,
    )
```
